256 devices in a mesh: dp: 32 (over x, y, core), mp: 8 (over z).
Axes of the slice: x: 4, y: 4, z: 8, core: 2. Of those that a mesh axis runs over, the one named last changes fastest.
Arguments:
- layer_input: bfloat16 [1024, 8192], P('dp'), may hold values from -12 to 12
- output_grad: bfloat16 [1024, 8192], P('dp'), may hold values from -24 to 24
- gate_pre: bfloat16 [1024, 32768], P('dp', 'mp'), may hold values from -4 to 4
- up_pre: bfloat16 [1024, 32768], P('dp', 'mp'), may hold values from -10 to 10
- hidden_grad: bfloat16 [1024, 32768], P('dp', 'mp'), may hold values from -22 to 22
- row_gate: float32 [8192], P('dp'), may hold values from 0.01 to 0.3
- col_gate: float32 [32768], P('mp'), may hold values from 0.01 to 0.3
- row_up: float32 [8192], P('dp'), may hold values from 0.01 to 0.3
- col_up: float32 [32768], P('mp'), may hold values from 0.01 to 0.3
- row_down: float32 [32768], P('mp'), may hold values from 0.01 to 0.3
- col_down: float32 [8192], P('dp'), may hold values from 0.01 to 0.3
Outputs:
- step_gate: bfloat16 [8192, 32768], P('dp', 'mp')
- step_up: bfloat16 [8192, 32768], P('dp', 'mp')
- step_down: bfloat16 [32768, 8192], P('mp', 'dp')
- new_row_gate: float32 [8192], P('dp')
- new_col_gate: float32 [32768], P('mp')
- new_row_up: float32 [8192], P('dp')
- new_col_up: float32 [32768], P('mp')
- new_row_down: float32 [32768], P('mp')
- new_col_down: float32 [8192], P('dp')
The draws below stay inside these ranges and needn't reach their ends.
All inputs are finite; a program needn't handle non-finite values.
Results may differ from the reference program's by a relative error of at most 0.0053.
Values may be sent and summed in bfloat16 or wider, within the bound.
No kernel may reach another device: no remote copies, remote signals or barrier semaphores. Data moves between devices by JAX's collectives and lax.ppermute only.
A program may use at most 128 MiB of HBM per device.

```python
import math
import jax
import jax.numpy as jnp
from jax import lax

D = 8192
FF = 32768
STEP = 8
TOKENS = 1024


def column_scale(key, columns):
    ramp = 1.0 + 2.0 * jnp.arange(columns, dtype=jnp.float32) / max(columns - 1, 1)
    spread = jnp.exp(jax.random.uniform(key, (columns,), jnp.float32, -math.log(2.0), math.log(2.0)))
    return ramp * spread


def scaled_noise(key, rows, columns, level):
    first, second = jax.random.split(key, 2)
    scale = level * column_scale(second, columns)
    noise = jax.random.truncated_normal(first, -4.0, 4.0, (rows, columns), jnp.float32)
    return (noise * scale[None, :]).astype(jnp.bfloat16)


def draw_layer_input(key, part):
    key = jax.random.fold_in(key, 11)
    return scaled_noise(key, TOKENS, D, 0.5)


def draw_output_grad(key, part):
    key = jax.random.fold_in(key, 23)
    return scaled_noise(key, TOKENS, D, 1.0)


def draw_up_pre(key, part):
    key = jax.random.fold_in(key, 37)
    return scaled_noise(key, TOKENS, FF, 0.4)


def draw_hidden_grad(key, part):
    key = jax.random.fold_in(key, 41)
    return scaled_noise(key, TOKENS, FF, 0.9)


def shard_levels(rng, dims, shards, low, top_value):
    level = 1.0
    for axis_at, blocks in shards:
        steps = jax.random.uniform(jax.random.fold_in(jax.random.fold_in(rng, 6), axis_at), (blocks,), jnp.float32, low / len(shards), top_value / len(shards))
        level = level * jnp.repeat(jnp.exp(steps), dims[axis_at] // blocks).reshape((-1,) + (1,) * (len(dims) - 1 - axis_at))
    return level


def centred(own_key, dims, deviation, most, cuts=(), held_as=jnp.bfloat16):
    result = deviation * jax.random.normal(own_key, dims, jnp.float32)
    if cuts:
        result = result * shard_levels(own_key, dims, cuts, -0.22, 0.18)
    return jnp.clip(result, -most, most).astype(held_as)


def setup_inputs(seed: int = 0) -> dict:
    arg_keys = jax.random.split(jax.random.key(seed), 12)
    layer_input = draw_layer_input(jax.random.fold_in(arg_keys[11], 71), 0)
    output_grad = draw_output_grad(jax.random.fold_in(arg_keys[11], 71), 0)
    gate_pre = centred(arg_keys[2], (TOKENS, FF), 1.0, 4.0, ((0, 32), (1, 8)))
    up_pre = draw_up_pre(jax.random.fold_in(arg_keys[11], 71), 0)
    hidden_grad = draw_hidden_grad(jax.random.fold_in(arg_keys[11], 71), 0)
    row_gate = jnp.clip(jnp.exp(math.log(0.3) - 3.4011974 * jax.random.uniform(arg_keys[5], (D,), jnp.float32) ** shard_levels(arg_keys[5], (D,), ((0, 32),), -0.2, 0.2)), 0.01, 0.3)
    col_gate = jnp.clip(jnp.exp(math.log(0.3) - 3.4011974 * jax.random.uniform(arg_keys[6], (FF,), jnp.float32) ** shard_levels(arg_keys[6], (FF,), ((0, 8),), -0.2, 0.2)), 0.01, 0.3)
    row_up = jnp.clip(jnp.exp(math.log(0.3) - 3.4011974 * jax.random.uniform(arg_keys[7], (D,), jnp.float32) ** shard_levels(arg_keys[7], (D,), ((0, 32),), -0.2, 0.2)), 0.01, 0.3)
    col_up = jnp.clip(jnp.exp(math.log(0.3) - 3.4011974 * jax.random.uniform(arg_keys[8], (FF,), jnp.float32) ** shard_levels(arg_keys[8], (FF,), ((0, 8),), -0.2, 0.2)), 0.01, 0.3)
    row_down = jnp.clip(jnp.exp(math.log(0.3) - 3.4011974 * jax.random.uniform(arg_keys[9], (FF,), jnp.float32) ** shard_levels(arg_keys[9], (FF,), ((0, 8),), -0.2, 0.2)), 0.01, 0.3)
    col_down = jnp.clip(jnp.exp(math.log(0.3) - 3.4011974 * jax.random.uniform(arg_keys[10], (D,), jnp.float32) ** shard_levels(arg_keys[10], (D,), ((0, 32),), -0.2, 0.2)), 0.01, 0.3)
    return {"layer_input": layer_input, "output_grad": output_grad, "gate_pre": gate_pre, "up_pre": up_pre, "hidden_grad": hidden_grad, "row_gate": row_gate, "col_gate": col_gate, "row_up": row_up, "col_up": col_up, "row_down": row_down, "col_down": col_down}


eps_square = 1e-30

def derive(gate_pre, up_pre, hidden_grad):
    first = gate_pre.astype(jnp.float32)
    second = up_pre.astype(jnp.float32)
    cotangent = hidden_grad.astype(jnp.float32)
    sigma = jax.nn.sigmoid(first)
    gate_cot = (cotangent * second * sigma * (1.0 + first * (1.0 - sigma))).astype(jnp.bfloat16)
    up_cot = (cotangent * first * sigma).astype(jnp.bfloat16)
    hidden = (first * sigma * second).astype(jnp.bfloat16)
    return (gate_cot, up_cot, hidden)

def factored(grad, row_old, col_old):
    beta = 1.0 - float(STEP) ** (-0.8)
    count_rows = grad.shape[0]
    count_cols = grad.shape[1]
    block = min(512, count_rows)
    starts = jnp.arange(count_rows // block, dtype=jnp.int32) * block

    def take(start):
        return lax.dynamic_slice_in_dim(grad, start, block, 0)

    def moments(start):
        piece = take(start)
        square = piece * piece
        return (lax.optimization_barrier(jnp.sum(square, axis=1)), lax.optimization_barrier(jnp.sum(square, axis=0)))
    row_parts, col_parts = lax.map(moments, starts)
    new_row = beta * row_old + (1.0 - beta) * (row_parts.reshape(count_rows) / count_cols + eps_square)
    new_col = beta * col_old + (1.0 - beta) * (lax.optimization_barrier(jnp.sum(col_parts, axis=0)) / count_rows + eps_square)
    row_scale = lax.rsqrt(new_row)
    col_scale = lax.rsqrt(new_col)

    def normed_block(start):
        piece = take(start)
        scales = lax.dynamic_slice_in_dim(row_scale, start, block, 0)
        return piece * scales[:, None] * col_scale[None, :]

    def squares(start):
        normed = normed_block(start)
        return jnp.sum(normed * normed)
    spread = jnp.sqrt(jnp.sum(lax.map(squares, starts)) / (count_rows * count_cols))
    divisor = jnp.maximum(1.0, spread)

    def output(start):
        return (normed_block(start) / divisor).astype(jnp.bfloat16)
    update = lax.map(output, starts).reshape(count_rows, count_cols)
    return (update, new_row, new_col)

def reference(layer_input, output_grad, gate_pre, up_pre, hidden_grad, row_gate, col_gate, row_up, col_up, row_down, col_down):
    gate_cot, up_cot, hidden = derive(gate_pre, up_pre, hidden_grad)
    factor = 1.0 / math.sqrt(TOKENS)
    grad_gate = jnp.dot(layer_input.T, gate_cot, preferred_element_type=jnp.float32) * factor
    step_gate, new_row_gate, new_col_gate = factored(grad_gate, row_gate, col_gate)
    grad_gate = None
    grad_up = jnp.dot(layer_input.T, up_cot, preferred_element_type=jnp.float32) * factor
    step_up, new_row_up, new_col_up = factored(grad_up, row_up, col_up)
    grad_up = None
    grad_down = jnp.dot(hidden.T, output_grad, preferred_element_type=jnp.float32) * factor
    step_down, new_row_down, new_col_down = factored(grad_down, row_down, col_down)
    return (step_gate, step_up, step_down, new_row_gate, new_col_gate, new_row_up, new_col_up, new_row_down, new_col_down)
```

```python
import functools

import jax
import jax.numpy as jnp
from jax import lax
from jax.experimental import pallas as pl
from jax.experimental.pallas import tpu as pltpu
from jax.sharding import Mesh, PartitionSpec as P

D = 8192
FF = 32768
STEP = 8
TOKENS = 1024

EPS = 1e-30
BETA = 1.0 - float(STEP) ** (-0.8)
XN, YN, CN, ZN = 4, 4, 2, 8
ROWS = D // (XN * YN * CN)
COLS = FF // ZN
HALF = COLS // 2
QUART = HALF // 2
LOCAL = TOKENS // (XN * YN * CN)
ORDER = (0, 3, 1, 2)
VMEM = 56 * 1024 * 1024


def derive(gate_pre, up_pre, hidden_grad):
    first = gate_pre.astype(jnp.float32)
    second = up_pre.astype(jnp.float32)
    cotangent = hidden_grad.astype(jnp.float32)
    sigma = jax.nn.sigmoid(first)
    gate_cot = (cotangent * second * sigma * (1.0 + first * (1.0 - sigma))).astype(jnp.bfloat16)
    up_cot = (cotangent * first * sigma).astype(jnp.bfloat16)
    hidden = (first * sigma * second).astype(jnp.bfloat16)
    return jnp.stack((gate_cot, up_cot, hidden))


def shift(value, axis, size, step):
    return lax.ppermute(value, axis, [(i, (i + step) % size) for i in range(size)])


def swap(value):
    return shift(value, "c", CN, 1)


def neighbours(value, axis):
    return shift(value, axis, 4, 1), shift(value, axis, 4, 3)


def relay(left, right, axis):
    return shift(left, axis, 4, 1), shift(right, axis, 4, 3)


def spread(value, axes, count):
    sent = jnp.broadcast_to(value[None], (count,) + value.shape)
    return lax.all_to_all(sent, axes, split_axis=0, concat_axis=0, tiled=True)


def multiply_kernel(xa_ref, xb_ref, *refs):
    a_refs, b_refs = refs[0:5], refs[5:10]
    keep_ref, send_ref, rows_ref, cols_ref = refs[10:]
    tile = QUART // 2
    rows = jnp.zeros((2 * ROWS, 1), jnp.float32)
    for route, (x_ref, (own, left, right, low, high)) in enumerate(((xa_ref, a_refs), (xb_ref, b_refs))):
        for part in range(2):
            at = pl.ds(part * tile, tile)
            far = (low, high)[part]
            total = jnp.zeros((2 * ROWS, tile), jnp.float32)
            for block, ref in enumerate((own, left, right)):
                total += jnp.dot(
                    x_ref[0, :, pl.ds(block * 256, 256)], ref[0, :, at], preferred_element_type=jnp.float32
                )
            total += jnp.dot(x_ref[0, :, pl.ds(768, 256)], far[0], preferred_element_type=jnp.float32)
            grad = total * (1.0 / 32.0)
            square = grad * grad
            rows += jnp.sum(square, axis=1, keepdims=True)
            place = pl.ds(route * QUART + part * tile, tile)
            cols_ref[0, :, place] = jnp.sum(square, axis=0, keepdims=True)
            rounded = grad.astype(jnp.bfloat16)
            keep_ref[0, :, place] = rounded[:ROWS]
            send_ref[0, :, place] = rounded[ROWS:]
    rows_ref[0] = rows


def multiply(xa, xb, a_parts, b_parts):
    def part_spec(width):
        return pl.BlockSpec((1, 256, width), lambda m: (m, 0, 0))

    x_spec = pl.BlockSpec((1, 2 * ROWS, TOKENS), lambda m: (m // 2, 0, 0))
    widths = (QUART, QUART, QUART, QUART // 2, QUART // 2)
    return pl.pallas_call(
        multiply_kernel,
        grid=(3,),
        in_specs=[x_spec, x_spec] + [part_spec(w) for w in widths + widths],
        out_specs=[
            pl.BlockSpec((1, ROWS, HALF), lambda m: (m, 0, 0)),
            pl.BlockSpec((1, ROWS, HALF), lambda m: (m, 0, 0)),
            pl.BlockSpec((1, 2 * ROWS, 1), lambda m: (m, 0, 0)),
            pl.BlockSpec((1, 1, HALF), lambda m: (m, 0, 0)),
        ],
        out_shape=[
            jax.ShapeDtypeStruct((3, ROWS, HALF), jnp.bfloat16),
            jax.ShapeDtypeStruct((3, ROWS, HALF), jnp.bfloat16),
            jax.ShapeDtypeStruct((3, 2 * ROWS, 1), jnp.float32),
            jax.ShapeDtypeStruct((3, 1, HALF), jnp.float32),
        ],
        compiler_params=pltpu.CompilerParams(vmem_limit_bytes=VMEM),
        cost_estimate=pl.CostEstimate(
            flops=3 * 2 * 2 * ROWS * HALF * TOKENS, bytes_accessed=24 << 20, transcendentals=0
        ),
        name="multiply",
    )(xa, xb, *a_parts, *b_parts)


def weigh_kernel(core_ref, keep_ref, got_ref, inverse_ref, out_ref):
    core = core_ref[0]
    total = jnp.zeros((ROWS, 1), jnp.float32)
    for ref, at in ((keep_ref, core), (got_ref, 1 - core)):
        grad = ref[0].astype(jnp.float32)
        total += jnp.sum(grad * grad * inverse_ref[at, 0], axis=1, keepdims=True)
    out_ref[0] = total


def weigh(core, keep, got, inverse):
    block = pl.BlockSpec((1, ROWS, HALF), lambda m, core: (m, 0, 0))
    return pl.pallas_call(
        weigh_kernel,
        grid_spec=pltpu.PrefetchScalarGridSpec(
            num_scalar_prefetch=1,
            grid=(3,),
            in_specs=[block, block, pl.BlockSpec((2, 1, 1, HALF), lambda m, core: (0, m, 0, 0))],
            out_specs=pl.BlockSpec((1, ROWS, 1), lambda m, core: (m, 0, 0)),
        ),
        out_shape=jax.ShapeDtypeStruct((3, ROWS, 1), jnp.float32),
        compiler_params=pltpu.CompilerParams(vmem_limit_bytes=VMEM),
        cost_estimate=pl.CostEstimate(flops=12 * ROWS * COLS, bytes_accessed=6 << 20, transcendentals=0),
        name="weigh",
    )(core, keep, got, inverse)


def finish_kernel(core_ref, keep_ref, got_ref, width_ref, unit_ref, gate_ref, up_ref, down_ref):
    core = core_ref[0]
    for m, out_ref in enumerate((gate_ref, up_ref, down_ref)):
        for ref, at in ((keep_ref, core), (got_ref, 1 - core)):
            normed = ref[m].astype(jnp.float32) * width_ref[m] * unit_ref[at, m]
            place = pl.ds(pl.multiple_of(at * HALF, HALF), HALF)
            if m < 2:
                out_ref[:, place] = normed.astype(jnp.bfloat16)
            else:
                out_ref[place, :] = normed.astype(jnp.bfloat16).T


def finish(core, keep, got, width, unit):
    tile = 128
    block = pl.BlockSpec((3, tile, HALF), lambda i, core: (0, i, 0))
    return pl.pallas_call(
        finish_kernel,
        grid_spec=pltpu.PrefetchScalarGridSpec(
            num_scalar_prefetch=1,
            grid=(ROWS // tile,),
            in_specs=[
                block,
                block,
                pl.BlockSpec((3, tile, 1), lambda i, core: (0, i, 0)),
                pl.BlockSpec((2, 3, 1, HALF), lambda i, core: (0, 0, 0, 0)),
            ],
            out_specs=[
                pl.BlockSpec((tile, COLS), lambda i, core: (i, 0)),
                pl.BlockSpec((tile, COLS), lambda i, core: (i, 0)),
                pl.BlockSpec((COLS, tile), lambda i, core: (0, i)),
            ],
        ),
        out_shape=[
            jax.ShapeDtypeStruct((ROWS, COLS), jnp.bfloat16),
            jax.ShapeDtypeStruct((ROWS, COLS), jnp.bfloat16),
            jax.ShapeDtypeStruct((COLS, ROWS), jnp.bfloat16),
        ],
        compiler_params=pltpu.CompilerParams(vmem_limit_bytes=VMEM),
        cost_estimate=pl.CostEstimate(flops=12 * ROWS * COLS, bytes_accessed=12 << 20, transcendentals=0),
        name="finish",
    )(core, keep, got, width, unit)


def turn(value, axis, start, size):
    return lax.dynamic_slice_in_dim(jnp.concatenate((value, value), axis), start, size, axis)


def features(layer_input, output_grad, x, y, c):
    both = jnp.stack((layer_input, output_grad)).reshape(2, LOCAL, XN * YN, 2 * ROWS)
    sent = both.transpose(2, 0, 1, 3)
    mine = lax.all_to_all(sent, ("x", "y"), split_axis=0, concat_axis=0, tiled=True)
    other = swap(mine)
    all_tokens = jnp.stack((mine, other), axis=1).reshape(XN, YN, 2, 2, LOCAL, 2, ROWS)
    all_tokens = turn(all_tokens, 0, x, XN)
    all_tokens = turn(all_tokens, 1, y, YN)
    all_tokens = turn(all_tokens, 5, c, CN)
    ordered = jnp.stack([all_tokens[d] for d in ORDER])
    ordered = jnp.stack([ordered[:, d] for d in ORDER], axis=1)
    by_x = ordered.transpose(3, 5, 6, 0, 1, 2, 4).reshape(2, 2 * ROWS, TOKENS)
    by_y = ordered.transpose(3, 5, 6, 1, 0, 2, 4).reshape(2, 2 * ROWS, TOKENS)
    return by_y, by_x


def gather(own, first, second):
    left, right = neighbours(own, first)
    half = LOCAL
    far_low, far_high = relay(left[:, :half], right[:, half:], first)
    line = jnp.concatenate((own, left, right, far_low, far_high), axis=1)
    left, right = neighbours(line, second)
    half = QUART // 2
    far_low, far_high = relay(left[:, :, :half], right[:, :, half:], second)
    return line, left, right, far_low, far_high


def local(
    layer_input,
    output_grad,
    gate_pre,
    up_pre,
    hidden_grad,
    row_gate,
    col_gate,
    row_up,
    col_up,
    row_down,
    col_down,
):
    x, y, c = lax.axis_index("x"), lax.axis_index("y"), lax.axis_index("c")
    core = c.astype(jnp.int32).reshape(1)

    def halves(at):
        return derive(*(lax.dynamic_slice_in_dim(v, at * HALF, HALF, 1) for v in (gate_pre, up_pre, hidden_grad)))

    got = swap(halves(1 - c))
    own = jnp.concatenate((halves(c), got), axis=1)
    a_parts = gather(own[:, :, :QUART], "x", "y")
    b_parts = gather(own[:, :, QUART:], "y", "x")
    xa, xb = features(layer_input, output_grad, x, y, c)
    keep, send, rows, cols = multiply(xa, xb, a_parts, b_parts)
    got = swap(send)
    rows_own = rows[:, :ROWS, 0] + swap(rows[:, ROWS:, 0])

    parts = spread(cols.reshape(1, 3 * HALF), ("x", "y", "c"), XN * YN * CN)
    span = jnp.sum(parts.reshape(XN * YN, CN, 3, HALF), axis=0)
    old = jnp.stack((col_gate, col_up, row_down)).reshape(3, CN, HALF).transpose(1, 0, 2)
    new_span = BETA * old + (1.0 - BETA) * (span / D + EPS)

    weighted = weigh(core, keep, got, (1.0 / new_span)[:, :, None, :])[:, :, 0]
    both = spread(jnp.concatenate((rows_own, weighted)).reshape(1, 6 * ROWS), ("z",), ZN)
    both = jnp.sum(both.reshape(ZN, 2, 3, ROWS), axis=0)
    new_width = BETA * jnp.stack((row_gate, row_up, col_down)) + (1.0 - BETA) * (both[0] / FF + EPS)
    squares = jnp.sum(both[1] / new_width, axis=1)
    squares = spread(jnp.broadcast_to(squares[:, None], (3, 128)).reshape(1, 3 * 128), ("x", "y", "c"), XN * YN * CN)
    squares = jnp.sum(squares.reshape(XN * YN * CN, 3, 128), axis=0)[:, :1]
    scale = 1.0 / jnp.maximum(1.0, jnp.sqrt(squares / (D * FF)))
    width = (lax.rsqrt(new_width) * scale)[:, :, None]
    unit = lax.rsqrt(new_span)[:, :, None, :]
    step_gate, step_up, step_down = finish(core, keep, got, width, unit)
    columns = new_span.transpose(1, 0, 2).reshape(3, COLS)
    return (
        step_gate,
        step_up,
        step_down,
        new_width[0],
        columns[0],
        new_width[1],
        columns[1],
        columns[2],
        new_width[2],
    )


def solution(mesh):
    grid = Mesh(mesh.devices.reshape(XN, YN, CN, ZN), ("x", "y", "c", "z"))
    dp = ("x", "y", "c")
    return jax.shard_map(
        local,
        mesh=grid,
        in_specs=(
            P(dp, None),
            P(dp, None),
            P(dp, "z"),
            P(dp, "z"),
            P(dp, "z"),
            P(dp),
            P("z"),
            P(dp),
            P("z"),
            P("z"),
            P(dp),
        ),
        out_specs=(
            P(dp, "z"),
            P(dp, "z"),
            P("z", dp),
            P(dp),
            P("z"),
            P(dp),
            P("z"),
            P("z"),
            P(dp),
        ),
        check_vma=False,
    )
```

```python
import functools

import jax
import jax.numpy as jnp
from jax import lax
from jax.experimental import pallas as pl
from jax.experimental.pallas import tpu as pltpu
from jax.sharding import Mesh, PartitionSpec as P

D = 8192
FF = 32768
STEP = 8
TOKENS = 1024

EPS = 1e-30
BETA = 1.0 - float(STEP) ** (-0.8)
XN, YN, CN, ZN = 4, 4, 2, 8
ROWS = D // (XN * YN * CN)
COLS = FF // ZN
HALF = COLS // 2
QUART = HALF // 2
LOCAL = TOKENS // (XN * YN * CN)
ORDER = (0, 3, 1, 2)
VMEM = 48 * 1024 * 1024
PIECES = (2, 1)
ARRAY = (0, 1)


def derive(gate_pre, up_pre, hidden_grad):
    first = gate_pre.astype(jnp.float32)
    second = up_pre.astype(jnp.float32)
    cotangent = hidden_grad.astype(jnp.float32)
    sigma = jax.nn.sigmoid(first)
    gate_cot = (cotangent * second * sigma * (1.0 + first * (1.0 - sigma))).astype(jnp.bfloat16)
    up_cot = (cotangent * first * sigma).astype(jnp.bfloat16)
    hidden = (first * sigma * second).astype(jnp.bfloat16)
    return jnp.stack((gate_cot, up_cot, hidden))


def shift(value, axis, size, step):
    return lax.ppermute(value, axis, [(i, (i + step) % size) for i in range(size)])


def swap(value):
    return shift(value, "c", CN, 1)


def neighbours(value, axis):
    return shift(value, axis, 4, 1), shift(value, axis, 4, 3)


def relay(left, right, axis):
    half = left.shape[0] // 2
    return shift(left[:half], axis, 4, 1), shift(right[half:], axis, 4, 3)


def spread(value, axes, count):
    sent = jnp.broadcast_to(value[None], (count,) + value.shape)
    return lax.all_to_all(sent, axes, split_axis=0, concat_axis=0, tiled=True)


def join_kernel(own, left, right, low, high, *rest):
    lines, sem = rest[:-1], rest[-1]
    copies = []
    start = 0
    for line in lines:
        mats = pl.ds(start, line.shape[2])
        for block, ref in enumerate((own, left, right)):
            copies.append((ref.at[:, mats], line.at[block]))
        for core, ref in enumerate((low, high)):
            copies.append((ref.at[0, mats], line.at[3, core]))
        start += line.shape[2]
    copies = [pltpu.make_async_copy(a, b, sem.at[i]) for i, (a, b) in enumerate(copies)]
    for copy in copies:
        copy.start()
    for copy in copies:
        copy.wait()


def join(own, left, right, low, high):
    return pl.pallas_call(
        join_kernel,
        in_specs=[pl.BlockSpec(memory_space=pl.ANY)] * 5,
        out_specs=[pl.BlockSpec(memory_space=pl.ANY)] * len(PIECES),
        out_shape=[jax.ShapeDtypeStruct((4, CN, n, LOCAL, QUART), jnp.bfloat16) for n in PIECES],
        scratch_shapes=[pltpu.SemaphoreType.DMA((5 * len(PIECES),))],
        cost_estimate=pl.CostEstimate(flops=0, bytes_accessed=3 << 20, transcendentals=0),
        name="join",
    )(own, left, right, low, high)


def multiply_kernel(xa_ref, xb_ref, *refs):
    a_refs, b_refs = refs[0:5], refs[5:10]
    keep_ref, send_ref, rows_ref, cols_ref = refs[10:]
    step = pl.program_id(1)
    tile = keep_ref.shape[3]
    across = jnp.zeros((2 * ROWS, 128), jnp.float32)
    for route, (x_ref, blocks) in enumerate(((xa_ref, a_refs), (xb_ref, b_refs))):
        total = jnp.zeros((2 * ROWS, tile), jnp.float32)
        at = 0
        for ref in blocks:
            depth = ref.shape[0] * CN * LOCAL
            block = ref[:, :, 0].reshape(depth, tile)
            total += jnp.dot(x_ref[0, :, at : at + depth], block, preferred_element_type=jnp.float32)
            at += depth
        grad = total * (1.0 / 32.0)
        square = grad * grad
        down = jnp.sum(square, axis=0, keepdims=True)
        for k in range(tile // 128):
            across += square[:, k * 128 : (k + 1) * 128]
            cols_ref[0, route, pl.ds(step * (tile // 128) + k, 1), :] = down[:, k * 128 : (k + 1) * 128]
        rounded = grad.astype(jnp.bfloat16)
        keep_ref[0, route] = rounded[:ROWS]
        send_ref[0, route] = rounded[ROWS:]
    across = jnp.sum(across.T, axis=0, keepdims=True)

    @pl.when(step == 0)
    def _():
        rows_ref[0] = across

    @pl.when(step > 0)
    def _():
        rows_ref[0] += across


def multiply(array, xa, xb, a_parts, b_parts):
    n = a_parts[0].shape[2]
    tile = QUART // 2

    def part_spec(part):
        return pl.BlockSpec((part.shape[0], CN, 1, LOCAL, tile), lambda m, t: (0, 0, m, 0, t))

    x_spec = pl.BlockSpec((1, 2 * ROWS, TOKENS), lambda m, t: (array, 0, 0))
    grad_spec = pl.BlockSpec((1, 2, ROWS, tile), lambda m, t: (m, 0, 0, t))
    return pl.pallas_call(
        multiply_kernel,
        grid=(n, QUART // tile),
        in_specs=[x_spec, x_spec] + [part_spec(p) for p in a_parts + b_parts],
        out_specs=[
            grad_spec,
            grad_spec,
            pl.BlockSpec((1, 1, 2 * ROWS), lambda m, t: (m, 0, 0)),
            pl.BlockSpec((1, 2, 8, 128), lambda m, t: (m, 0, 0, 0)),
        ],
        out_shape=[
            jax.ShapeDtypeStruct((n, 2, ROWS, QUART), jnp.bfloat16),
            jax.ShapeDtypeStruct((n, 2, ROWS, QUART), jnp.bfloat16),
            jax.ShapeDtypeStruct((n, 1, 2 * ROWS), jnp.float32),
            jax.ShapeDtypeStruct((n, 2, 8, 128), jnp.float32),
        ],
        compiler_params=pltpu.CompilerParams(vmem_limit_bytes=VMEM),
        cost_estimate=pl.CostEstimate(
            flops=n * 2 * 2 * ROWS * HALF * TOKENS, bytes_accessed=n * (8 << 20), transcendentals=0
        ),
        name="multiply",
    )(xa, xb, *a_parts, *b_parts)


def weigh_kernel(inverse_ref, *refs):
    out_ref = refs[-1]
    m = 0
    for keep_ref, send_ref in zip(refs[0:-1:2], refs[1:-1:2]):
        for i in range(keep_ref.shape[0]):
            for half, ref in enumerate((keep_ref, send_ref)):
                total = jnp.zeros((ref.shape[2], 128), jnp.float32)
                for route in range(2):
                    for k in range(8):
                        grad = ref[i, route, :, k * 128 : (k + 1) * 128].astype(jnp.float32)
                        total += grad * grad * inverse_ref[(m * 2 + route) * 8 + k][None]
                out_ref[m, half] = jnp.sum(total.T, axis=0)
            m += 1


def weigh(inverse, *grads):
    tile = 128

    def spec(grad):
        return pl.BlockSpec((grad.shape[0], 2, tile, QUART), lambda i: (0, 0, i, 0))

    return pl.pallas_call(
        weigh_kernel,
        grid=(ROWS // tile,),
        in_specs=[pl.BlockSpec((48, 128), lambda i: (0, 0))] + [spec(g) for g in grads],
        out_specs=pl.BlockSpec((3, 2, tile), lambda i: (0, 0, i)),
        out_shape=jax.ShapeDtypeStruct((3, 2, ROWS), jnp.float32),
        compiler_params=pltpu.CompilerParams(vmem_limit_bytes=VMEM),
        cost_estimate=pl.CostEstimate(flops=12 * ROWS * COLS, bytes_accessed=6 << 20, transcendentals=0),
        name="weigh",
    )(inverse, *grads)


def finish_kernel(core_ref, width_ref, mine_ref, other_ref, *refs):
    grads, outs = refs[:-3], refs[-3:]
    core = core_ref[0]
    m = 0
    for keep_ref, got_ref in zip(grads[0::2], grads[1::2]):
        for i in range(keep_ref.shape[0]):
            rows = keep_ref.shape[2]
            width = jnp.broadcast_to(width_ref[m][None], (128, rows)).T
            for ref, unit_ref, at in ((keep_ref, mine_ref, core), (got_ref, other_ref, 1 - core)):
                for route in range(2):
                    for k in range(8):
                        unit = unit_ref[(m * 2 + route) * 8 + k][None]
                        grad = ref[i, route, :, k * 128 : (k + 1) * 128].astype(jnp.float32)
                        normed = (grad * width * unit).astype(jnp.bfloat16)
                        place = pl.ds(pl.multiple_of(at * HALF + route * QUART + k * 128, 128), 128)
                        if m < 2:
                            outs[m][:, place] = normed
                        else:
                            outs[m][place, :] = normed.T
            m += 1


def finish(core, width, mine, other, *grads):
    tile = 128

    def spec(grad):
        return pl.BlockSpec((grad.shape[0], 2, tile, QUART), lambda i, core: (0, 0, i, 0))

    unit_spec = pl.BlockSpec((48, 128), lambda i, core: (0, 0))
    return pl.pallas_call(
        finish_kernel,
        grid_spec=pltpu.PrefetchScalarGridSpec(
            num_scalar_prefetch=1,
            grid=(ROWS // tile,),
            in_specs=[pl.BlockSpec((3, tile), lambda i, core: (0, i)), unit_spec, unit_spec] + [spec(g) for g in grads],
            out_specs=[
                pl.BlockSpec((tile, COLS), lambda i, core: (i, 0)),
                pl.BlockSpec((tile, COLS), lambda i, core: (i, 0)),
                pl.BlockSpec((COLS, tile), lambda i, core: (0, i)),
            ],
        ),
        out_shape=[
            jax.ShapeDtypeStruct((ROWS, COLS), jnp.bfloat16),
            jax.ShapeDtypeStruct((ROWS, COLS), jnp.bfloat16),
            jax.ShapeDtypeStruct((COLS, ROWS), jnp.bfloat16),
        ],
        compiler_params=pltpu.CompilerParams(vmem_limit_bytes=VMEM),
        cost_estimate=pl.CostEstimate(flops=12 * ROWS * COLS, bytes_accessed=12 << 20, transcendentals=0),
        name="finish",
    )(core, width, mine, other, *grads)


def arrange_kernel(place_ref, mine_ref, other_ref, a_ref, b_ref):
    x, y, c = place_ref[0], place_ref[1], place_ref[2]
    for part in range(4):
        column = lax.rem(c + part // 2, 2) * 2 + part % 2
        for out_ref, by_x in ((a_ref, False), (b_ref, True)):
            for outer, d in enumerate(ORDER):
                blocks = []
                for e in ORDER:
                    dx, dy = (d, e) if by_x else (e, d)
                    source = lax.rem(x + dx, XN) * YN + lax.rem(y + dy, YN)
                    blocks += [mine_ref[column, source], other_ref[column, source]]
                out_ref[0, part * 128 : (part + 1) * 128, outer * 256 : (outer + 1) * 256] = jnp.concatenate(blocks).T


def arrange(place, mine, other):
    spec = pl.BlockSpec((4, XN * YN, LOCAL, 128), lambda i, place: (i, 0, 0, 0))
    out_spec = pl.BlockSpec((1, 2 * ROWS, TOKENS), lambda i, place: (i, 0, 0))
    out = jax.ShapeDtypeStruct((2, 2 * ROWS, TOKENS), jnp.bfloat16)
    return pl.pallas_call(
        arrange_kernel,
        grid_spec=pltpu.PrefetchScalarGridSpec(
            num_scalar_prefetch=1, grid=(2,), in_specs=[spec, spec], out_specs=[out_spec, out_spec]
        ),
        out_shape=[out, out],
        compiler_params=pltpu.CompilerParams(vmem_limit_bytes=VMEM),
        cost_estimate=pl.CostEstimate(flops=0, bytes_accessed=6 << 20, transcendentals=0),
        name="arrange",
    )(place, mine, other)


def features(chosen, place, z):
    chosen = chosen.reshape(LOCAL, XN * YN, 4, 128)
    sent = lax.dynamic_index_in_dim(chosen, lax.rem(z, 4), 2, keepdims=False).transpose(1, 0, 2)
    part = lax.all_to_all(sent, ("x", "y"), split_axis=0, concat_axis=0, tiled=True)
    mine = lax.all_gather(part, "z")
    return arrange(place, mine, swap(mine))


def local(
    layer_input,
    output_grad,
    gate_pre,
    up_pre,
    hidden_grad,
    row_gate,
    col_gate,
    row_up,
    col_up,
    row_down,
    col_down,
):
    x, y, c, z = (lax.axis_index(name) for name in ("x", "y", "c", "z"))
    core = c.astype(jnp.int32).reshape(1)
    place = jnp.stack((x, y, c)).astype(jnp.int32)

    def halves(at):
        return derive(*(lax.dynamic_slice_in_dim(v, at * HALF, HALF, 1) for v in (gate_pre, up_pre, hidden_grad)))

    got = swap(halves(1 - c))
    own = jnp.stack((halves(c), got))
    own_a, own_b = own[..., :QUART], own[..., QUART:]
    chosen = jnp.where(z < 4, layer_input, output_grad)
    own_a, own_b, chosen = lax.optimization_barrier((own_a, own_b, chosen))

    ring = []
    for own, first in ((own_a, "x"), (own_b, "y")):
        left, right = neighbours(own, first)
        ring.append((own, left, right))
    lines = []
    for (own, left, right), first in zip(ring, ("x", "y")):
        lines.append(join(own, left, right, *relay(left, right, first)))
    xa, xb = features(chosen, place, z)
    near = [[neighbours(lines[r][p], axis) for r, axis in ((0, "y"), (1, "x"))] for p in range(len(PIECES))]
    grads = []
    for p in range(len(PIECES)):
        parts = []
        for r, axis in ((0, "y"), (1, "x")):
            left, right = near[p][r]
            parts.append((lines[r][p], left, right) + relay(left, right, axis))
        grads.append(multiply(ARRAY[p], xa, xb, *parts))

    keeps, sends, rows, cols = zip(*grads)
    rows = jnp.concatenate(rows).reshape(3, 2, ROWS)
    cols = jnp.concatenate(cols).reshape(48, 128)
    gots = [swap(send) for send in sends]

    span = jnp.sum(spread(cols, ("x", "y"), XN * YN), axis=0)
    old = jnp.stack((col_gate, col_up, row_down)).reshape(3, CN, 16, 128)
    old = lax.dynamic_index_in_dim(old, c, 1, keepdims=False).reshape(48, 128)
    new_span = BETA * old + (1.0 - BETA) * (span / D + EPS)
    other_span = swap(new_span)

    weighted = weigh(1.0 / new_span, *(g for pair in zip(keeps, sends) for g in pair))
    both = jnp.concatenate((rows, weighted))
    both = both[:, 0] + swap(both[:, 1])
    both = jnp.sum(spread(both, ("z",), ZN), axis=0)
    new_width = BETA * jnp.stack((row_gate, row_up, col_down)) + (1.0 - BETA) * (both[:3] / FF + EPS)
    squares = jnp.sum(both[3:] / new_width, axis=1, keepdims=True)
    squares = jnp.sum(spread(jnp.broadcast_to(squares, (3, 128)), ("x", "y", "c"), XN * YN * CN), axis=0)[:, :1]
    scale = 1.0 / jnp.maximum(1.0, jnp.sqrt(squares / (D * FF)))
    width = lax.rsqrt(new_width) * scale
    step_gate, step_up, step_down = finish(
        core,
        width,
        lax.rsqrt(new_span),
        lax.rsqrt(other_span),
        *(g for pair in zip(keeps, gots) for g in pair),
    )
    mine, other = new_span.reshape(3, HALF), other_span.reshape(3, HALF)
    columns = jnp.where(c == 0, jnp.concatenate((mine, other), 1), jnp.concatenate((other, mine), 1))
    return (
        step_gate,
        step_up,
        step_down,
        new_width[0],
        columns[0],
        new_width[1],
        columns[1],
        columns[2],
        new_width[2],
    )


def solution(mesh):
    grid = Mesh(mesh.devices.reshape(XN, YN, CN, ZN), ("x", "y", "c", "z"))
    dp = ("x", "y", "c")
    return jax.shard_map(
        local,
        mesh=grid,
        in_specs=(
            P(dp, None),
            P(dp, None),
            P(dp, "z"),
            P(dp, "z"),
            P(dp, "z"),
            P(dp),
            P("z"),
            P(dp),
            P("z"),
            P("z"),
            P(dp),
        ),
        out_specs=(
            P(dp, "z"),
            P(dp, "z"),
            P("z", dp),
            P(dp),
            P("z"),
            P(dp),
            P("z"),
            P("z"),
            P(dp),
        ),
        check_vma=False,
    )
```

```python
import jax
import jax.numpy as jnp
from jax import lax
from jax.experimental import pallas as pl
from jax.experimental.pallas import tpu as pltpu
from jax.sharding import Mesh, PartitionSpec as P

D = 8192
FF = 32768
STEP = 8
TOKENS = 1024

EPS = 1e-30
BETA = 1.0 - float(STEP) ** (-0.8)
XN, YN, CN, ZN = 4, 4, 2, 8
ROWS = D // (XN * YN * CN)
COLS = FF // ZN
HALF = COLS // 2
QUART = HALF // 2
LOCAL = TOKENS // (XN * YN * CN)
VMEM = 12 * 1024 * 1024
SCALE = 1.0 / TOKENS
ORDER = (0, 3, 1, 2)


def derive(gate_pre, up_pre, hidden_grad):
    first = gate_pre.astype(jnp.float32)
    second = up_pre.astype(jnp.float32)
    cotangent = hidden_grad.astype(jnp.float32)
    sigma = jax.nn.sigmoid(first)
    gate_cot = (cotangent * second * sigma * (1.0 + first * (1.0 - sigma))).astype(jnp.bfloat16)
    up_cot = (cotangent * first * sigma).astype(jnp.bfloat16)
    hidden = (first * sigma * second).astype(jnp.bfloat16)
    return jnp.stack((gate_cot, up_cot, hidden))


def shift(value, axis, size, step):
    return lax.ppermute(value, axis, [(i, (i + step) % size) for i in range(size)])


def swap(value):
    return shift(value, "c", CN, 1)


def neighbours(value, axis):
    return shift(value, axis, 4, 1), shift(value, axis, 4, 3)


def here(*values):
    return [pltpu.with_memory_space_constraint(v, pltpu.VMEM) for v in values]


def whole(kernel, name, outs, operands, flops=0, scratch=()):
    size = sum(v.size * v.dtype.itemsize for v in operands)
    spec = pl.BlockSpec(memory_space=pltpu.VMEM)
    return pl.pallas_call(
        kernel,
        in_specs=[spec] * len(operands),
        out_specs=[spec] * len(outs),
        out_shape=[pltpu.VMEM(shape, dtype) for shape, dtype in outs],
        scratch_shapes=list(scratch),
        compiler_params=pltpu.CompilerParams(vmem_limit_bytes=VMEM),
        cost_estimate=pl.CostEstimate(flops=flops, bytes_accessed=size, transcendentals=0),
        name=name,
    )(*here(*operands))


def halve_kernel(*refs):
    for i in range(4):
        half = refs[4 + i].shape[0]
        refs[4 + i][...] = refs[i][i % 2 * half : (i % 2 + 1) * half]


def relay(pairs, axes):
    arrived = [v for pair in pairs for v in pair]
    outs = [((v.shape[0] // 2,) + v.shape[1:], v.dtype) for v in arrived]
    halves = whole(halve_kernel, "halve", outs, arrived)
    return [(shift(halves[2 * r], axis, 4, 1), shift(halves[2 * r + 1], axis, 4, 3)) for r, axis in enumerate(axes)]


def spread(value, axes, count):
    sent = jnp.broadcast_to(value[None], (count,) + value.shape)
    return lax.all_to_all(sent, axes, split_axis=0, concat_axis=0, tiled=True)


def join_kernel(*refs):
    for route in range(2):
        own, left, right, low, high = refs[5 * route : 5 * route + 5]
        line = refs[10 + route]
        for block, ref in enumerate((own, left, right)):
            line[block] = ref[...]
        line[3, 0] = low[0]
        line[3, 1] = high[0]


def join(blocks):
    return whole(join_kernel, "join", [((4, CN, 3, LOCAL, QUART), jnp.bfloat16)] * 2, blocks)


def pick_kernel(z_ref, first_ref, second_ref, out_ref):
    z = z_ref[0]
    for array, ref in enumerate((first_ref, second_ref)):

        @pl.when(z // 4 == array)
        def _():
            for chip in range(XN * YN):
                start = pl.multiple_of(chip * 2 * ROWS + lax.rem(z, 4) * 128, 128)
                out_ref[chip] = ref[:, pl.ds(start, 128)]


def pick(z, first, second):
    spec = pl.BlockSpec(memory_space=pltpu.VMEM)
    return pl.pallas_call(
        pick_kernel,
        in_specs=[pl.BlockSpec(memory_space=pltpu.SMEM), spec, spec],
        out_specs=spec,
        out_shape=jax.ShapeDtypeStruct((XN * YN, LOCAL, 128), jnp.bfloat16),
        compiler_params=pltpu.CompilerParams(vmem_limit_bytes=VMEM),
        cost_estimate=pl.CostEstimate(flops=0, bytes_accessed=1 << 20, transcendentals=0),
        name="pick",
    )(z, *here(first, second))


def start_kernel(*refs):
    features, parts, total_ref, line = refs[:4], refs[4:10], refs[10], refs[11]
    depth = line.shape[1]
    tile = line.shape[2]
    for m in range(3):
        for step in range(QUART // tile):
            units = slice(step * tile, (step + 1) * tile)
            for route in range(2):
                x_ref = features[m // 2 * 2 + route]
                size = depth // 3
                for i, ref in enumerate(parts[3 * route : 3 * route + 3]):
                    line[route, i * size : (i + 1) * size] = ref[:, :, m, :, units].reshape(size, tile)
                for i in range(2):
                    rows = slice(i * ROWS, (i + 1) * ROWS)
                    total_ref[m, route, rows, units] = jnp.dot(
                        x_ref[rows, :depth], line[route], preferred_element_type=jnp.float32
                    )


def start(features, parts):
    outs = [((3, 2, 2 * ROWS, QUART), jnp.float32)]
    depth = TOKENS * 3 // 4
    scratch = [pltpu.VMEM((2, depth, QUART // 2), jnp.bfloat16)]
    return whole(start_kernel, "start", outs, (*features, *parts), 3 * 4 * ROWS * HALF * depth, scratch)[0]


def multiply_kernel(*refs):
    features, total_ref, parts = refs[:4], refs[4], refs[5:9]
    keep_ref, send_ref, rows_ref, cols_ref, line = refs[9:]
    depth = line.shape[1]
    tile = line.shape[2]
    for m in range(3):
        across = [jnp.zeros((ROWS, 128), jnp.float32) for _ in range(2)]
        for step in range(QUART // tile):
            units = slice(step * tile, (step + 1) * tile)
            for route in range(2):
                x_ref = features[m // 2 * 2 + route]
                size = depth // 2
                for i, ref in enumerate(parts[2 * route : 2 * route + 2]):
                    line[route, i * size : (i + 1) * size] = ref[:, :, m, :, units].reshape(size, tile)
                down = jnp.zeros((1, tile), jnp.float32)
                for i, out_ref in enumerate((keep_ref, send_ref)):
                    rows = slice(i * ROWS, (i + 1) * ROWS)
                    last = jnp.dot(x_ref[rows, TOKENS - depth :], line[route], preferred_element_type=jnp.float32)
                    grad = total_ref[m, route, rows, units] + last
                    out_ref[m, route, :, units] = grad.astype(jnp.bfloat16)
                    square = grad * grad
                    down += jnp.sum(square, axis=0, keepdims=True)
                    for k in range(tile // 128):
                        across[i] += square[:, k * 128 : (k + 1) * 128]
                for k in range(tile // 128):
                    row = step * (tile // 128) + k
                    cols_ref[m, route, row : row + 1, :] = down[:, k * 128 : (k + 1) * 128] * SCALE
        for i, total in enumerate(across):
            rows_ref[m, i : i + 1] = jnp.sum(total.T, axis=0, keepdims=True) * SCALE


def multiply(features, total, parts):
    outs = [
        ((3, 2, ROWS, QUART), jnp.bfloat16),
        ((3, 2, ROWS, QUART), jnp.bfloat16),
        ((3, 2, ROWS), jnp.float32),
        ((3, 2, 8, 128), jnp.float32),
    ]
    depth = TOKENS // 4
    scratch = [pltpu.VMEM((2, depth, QUART // 2), jnp.bfloat16)]
    return whole(multiply_kernel, "multiply", outs, (*features, total, *parts), 3 * 4 * ROWS * HALF * depth, scratch)


def weigh_kernel(mine_ref, other_ref, keep_ref, got_ref, out_ref):
    for m in range(3):
        total = jnp.zeros((ROWS, 128), jnp.float32)
        for ref, inverse_ref in ((keep_ref, mine_ref), (got_ref, other_ref)):
            for route in range(2):
                for k in range(8):
                    at = (m * 2 + route) * 8 + k
                    grad = ref[m, route, :, k * 128 : (k + 1) * 128].astype(jnp.float32)
                    total += grad * grad * inverse_ref[at : at + 1]
        out_ref[m : m + 1] = jnp.sum(total.T, axis=0, keepdims=True) * SCALE


def weigh(*operands):
    return whole(weigh_kernel, "weigh", [((3, ROWS), jnp.float32)], operands, 12 * ROWS * COLS)[0]


def finish_kernel(core_ref, width_ref, mine_ref, other_ref, keep_ref, got_ref, *refs):
    outs, bufs, sem = refs[:3], refs[3:6], refs[6]
    core = core_ref[0]
    copies = []
    for m in range(3):
        width = jnp.broadcast_to(width_ref[m : m + 1], (128, ROWS)).T
        for ref, unit_ref, at in ((keep_ref, mine_ref, core), (got_ref, other_ref, 1 - core)):
            for route in range(2):
                first = at * HALF + route * QUART
                for k in range(8):
                    row = (m * 2 + route) * 8 + k
                    grad = ref[m, route, :, k * 128 : (k + 1) * 128].astype(jnp.float32)
                    normed = (grad * width * unit_ref[row : row + 1]).astype(jnp.bfloat16)
                    place = pl.ds(pl.multiple_of(first + k * 128, 128), 128)
                    if m < 2:
                        bufs[m][:, place] = normed
                    else:
                        bufs[m][place, :] = normed.T
                part = pl.ds(pl.multiple_of(first, QUART), QUART)
                ends = [v.at[:, part] if m < 2 else v.at[part] for v in (bufs[m], outs[m])]
                copies.append(pltpu.make_async_copy(*ends, sem.at[len(copies)]))
                copies[-1].start()
    for copy in copies:
        copy.wait()


def finish(core, *operands):
    spec = pl.BlockSpec(memory_space=pltpu.VMEM)
    wide, tall = (ROWS, COLS), (COLS, ROWS)
    operands = here(*operands)
    return pl.pallas_call(
        finish_kernel,
        in_specs=[pl.BlockSpec(memory_space=pltpu.SMEM)] + [spec] * len(operands),
        out_specs=[pl.BlockSpec(memory_space=pl.ANY)] * 3,
        out_shape=[jax.ShapeDtypeStruct(shape, jnp.bfloat16) for shape in (wide, wide, tall)],
        scratch_shapes=[pltpu.VMEM(shape, jnp.bfloat16) for shape in (wide, wide, tall)]
        + [pltpu.SemaphoreType.DMA((12,))],
        compiler_params=pltpu.CompilerParams(vmem_limit_bytes=2 * VMEM),
        cost_estimate=pl.CostEstimate(flops=12 * ROWS * COLS, bytes_accessed=12 << 20, transcendentals=0),
        name="finish",
    )(core, *operands)


def arrange_kernel(place_ref, mine_ref, other_ref, *outs):
    x, y, core = place_ref[0], place_ref[1], place_ref[2]
    for array in range(2):
        for part in range(4):
            column = array * 4 + lax.rem(core + part // 2, 2) * 2 + part % 2
            rows = slice(part * 128, (part + 1) * 128)
            for route in range(2):
                for outer in range(4):
                    blocks = []
                    for inner in range(4):
                        dx, dy = (ORDER[outer], ORDER[inner]) if route else (ORDER[inner], ORDER[outer])
                        source = lax.rem(x + dx, XN) * YN + lax.rem(y + dy, YN)
                        blocks += [mine_ref[column, source], other_ref[column, source]]
                    tokens = slice(outer * 256, (outer + 1) * 256)
                    outs[array * 2 + route][rows, tokens] = jnp.concatenate(blocks).T


def arrange(place, mine, other):
    spec = pl.BlockSpec(memory_space=pltpu.VMEM)
    return pl.pallas_call(
        arrange_kernel,
        in_specs=[pl.BlockSpec(memory_space=pltpu.SMEM), spec, spec],
        out_specs=[spec] * 4,
        out_shape=[pltpu.VMEM((2 * ROWS, TOKENS), jnp.bfloat16)] * 4,
        compiler_params=pltpu.CompilerParams(vmem_limit_bytes=VMEM),
        cost_estimate=pl.CostEstimate(flops=0, bytes_accessed=6 << 20, transcendentals=0),
        name="arrange",
    )(place, *here(mine, other))


def local(
    layer_input,
    output_grad,
    gate_pre,
    up_pre,
    hidden_grad,
    row_gate,
    col_gate,
    row_up,
    col_up,
    row_down,
    col_down,
):
    x, y, c, z = (lax.axis_index(name) for name in ("x", "y", "c", "z"))
    core = c.astype(jnp.int32).reshape(1)
    place = jnp.stack((x, y, c)).astype(jnp.int32)

    def halves(at):
        return derive(*(lax.dynamic_slice_in_dim(v, at * HALF, HALF, 1) for v in (gate_pre, up_pre, hidden_grad)))

    got = swap(halves(1 - c))
    own = jnp.stack((halves(c), got))
    own_a, own_b = own[..., :QUART], own[..., QUART:]
    near = [neighbours(own_a, "x"), neighbours(own_b, "y")]

    chosen = pick(z.astype(jnp.int32).reshape(1), layer_input, output_grad)
    chosen = lax.all_to_all(chosen, ("x", "y"), split_axis=0, concat_axis=0, tiled=True)
    near, chosen = lax.optimization_barrier((near, chosen))
    far = relay(near, ("x", "y"))
    chosen = lax.all_gather(chosen, "z")
    lines = join([own_a, *near[0], *far[0], own_b, *near[1], *far[1]])

    near = [neighbours(line, axis) for line, axis in zip(lines, ("y", "x"))]
    far = relay(near, ("y", "x"))
    features = arrange(place, chosen, swap(chosen))
    parts = [lines[0], *near[0], lines[1], *near[1]]
    keep, send, rows, cols = multiply(features, start(features, parts), [*far[0], *far[1]])

    rows = rows[:, 0] + swap(rows[:, 1])
    cols = cols.reshape(48, 128)
    got = swap(send)

    span = jnp.sum(spread(cols, ("x", "y"), XN * YN), axis=0)
    old = jnp.stack((col_gate, col_up, row_down)).reshape(3, CN, 16, 128)
    old = lax.dynamic_index_in_dim(old, c, 1, keepdims=False).reshape(48, 128)
    new_span = BETA * old + (1.0 - BETA) * (span / D + EPS)
    other_span = swap(new_span)

    weighted = weigh(1.0 / new_span, 1.0 / other_span, keep, got)
    both = jnp.sum(spread(jnp.concatenate((rows, weighted)), ("z",), ZN), axis=0)
    new_width = BETA * jnp.stack((row_gate, row_up, col_down)) + (1.0 - BETA) * (both[:3] / FF + EPS)
    squares = jnp.sum(both[3:] / new_width, axis=1, keepdims=True)
    squares = jnp.sum(spread(jnp.broadcast_to(squares, (3, 128)), ("x", "y", "c"), XN * YN * CN), axis=0)[:, :1]
    scale = (1.0 / 32.0) / jnp.maximum(1.0, jnp.sqrt(squares / (D * FF)))
    width = lax.rsqrt(new_width) * scale
    step_gate, step_up, step_down = finish(
        core,
        width,
        lax.rsqrt(new_span),
        lax.rsqrt(other_span),
        keep,
        got,
    )
    mine, other = new_span.reshape(3, HALF), other_span.reshape(3, HALF)
    columns = jnp.where(c == 0, jnp.concatenate((mine, other), 1), jnp.concatenate((other, mine), 1))
    return (
        step_gate,
        step_up,
        step_down,
        new_width[0],
        columns[0],
        new_width[1],
        columns[1],
        columns[2],
        new_width[2],
    )


def solution(mesh):
    grid = Mesh(mesh.devices.reshape(XN, YN, CN, ZN), ("x", "y", "c", "z"))
    dp = ("x", "y", "c")
    return jax.shard_map(
        local,
        mesh=grid,
        in_specs=(
            P(dp, None),
            P(dp, None),
            P(dp, "z"),
            P(dp, "z"),
            P(dp, "z"),
            P(dp),
            P("z"),
            P(dp),
            P("z"),
            P("z"),
            P(dp),
        ),
        out_specs=(
            P(dp, "z"),
            P(dp, "z"),
            P("z", dp),
            P(dp),
            P("z"),
            P(dp),
            P("z"),
            P("z"),
            P(dp),
        ),
        check_vma=False,
    )
```

```python
import jax
import jax.numpy as jnp
from jax import lax
from jax.experimental import pallas as pl
from jax.experimental.pallas import tpu as pltpu
from jax.sharding import Mesh, PartitionSpec as P

D = 8192
FF = 32768
STEP = 8
TOKENS = 1024

EPS = 1e-30
BETA = 1.0 - float(STEP) ** (-0.8)
XN, YN, CN, ZN = 4, 4, 2, 8
ROWS = D // (XN * YN * CN)
COLS = FF // ZN
HALF = COLS // 2
QUART = HALF // 2
LOCAL = TOKENS // (XN * YN * CN)
VMEM = 12 * 1024 * 1024
SCALE = 1.0 / TOKENS
ORDER = (0, 3, 1, 2)


def derive(gate_pre, up_pre, hidden_grad):
    first = gate_pre.astype(jnp.float32)
    second = up_pre.astype(jnp.float32)
    cotangent = hidden_grad.astype(jnp.float32)
    sigma = jax.nn.sigmoid(first)
    gate_cot = (cotangent * second * sigma * (1.0 + first * (1.0 - sigma))).astype(jnp.bfloat16)
    up_cot = (cotangent * first * sigma).astype(jnp.bfloat16)
    hidden = (first * sigma * second).astype(jnp.bfloat16)
    return jnp.stack((gate_cot, up_cot, hidden))


def shift(value, axis, size, step):
    return lax.ppermute(value, axis, [(i, (i + step) % size) for i in range(size)])


def swap(value):
    return shift(value, "c", CN, 1)


def neighbours(value, axis):
    return shift(value, axis, 4, 1), shift(value, axis, 4, 3)


def here(*values):
    return [pltpu.with_memory_space_constraint(v, pltpu.VMEM) for v in values]


def whole(kernel, name, outs, operands, flops=0, scratch=()):
    size = sum(v.size * v.dtype.itemsize for v in operands)
    spec = pl.BlockSpec(memory_space=pltpu.VMEM)
    return pl.pallas_call(
        kernel,
        in_specs=[spec] * len(operands),
        out_specs=[spec] * len(outs),
        out_shape=[pltpu.VMEM(shape, dtype) for shape, dtype in outs],
        scratch_shapes=list(scratch),
        compiler_params=pltpu.CompilerParams(vmem_limit_bytes=VMEM),
        cost_estimate=pl.CostEstimate(flops=flops, bytes_accessed=size, transcendentals=0),
        name=name,
    )(*here(*operands))


def halve_kernel(*refs):
    for i in range(4):
        half = refs[4 + i].shape[0]
        refs[4 + i][...] = refs[i][i % 2 * half : (i % 2 + 1) * half]


def relay(pairs, axes):
    arrived = [v for pair in pairs for v in pair]
    outs = [((v.shape[0] // 2,) + v.shape[1:], v.dtype) for v in arrived]
    halves = whole(halve_kernel, "halve", outs, arrived)
    return [(shift(halves[2 * r], axis, 4, 1), shift(halves[2 * r + 1], axis, 4, 3)) for r, axis in enumerate(axes)]


def collect(copies, axes):
    return lax.all_to_all(copies, axes, split_axis=0, concat_axis=0, tiled=True)


def join_kernel(*refs):
    for route in range(2):
        own, left, right, low, high = refs[5 * route : 5 * route + 5]
        line = refs[10 + route]
        for block, ref in enumerate((own, left, right)):
            line[block] = ref[...]
        line[3, 0] = low[0]
        line[3, 1] = high[0]


def join(blocks):
    return whole(join_kernel, "join", [((4, CN, 3, LOCAL, QUART), jnp.bfloat16)] * 2, blocks)


def pick_kernel(z_ref, first_ref, second_ref, out_ref):
    z = z_ref[0]
    for array, ref in enumerate((first_ref, second_ref)):

        @pl.when(z // 4 == array)
        def _():
            for chip in range(XN * YN):
                start = pl.multiple_of(chip * 2 * ROWS + lax.rem(z, 4) * 128, 128)
                out_ref[chip] = ref[:, pl.ds(start, 128)]


def pick(z, first, second):
    spec = pl.BlockSpec(memory_space=pltpu.VMEM)
    return pl.pallas_call(
        pick_kernel,
        in_specs=[pl.BlockSpec(memory_space=pltpu.SMEM), spec, spec],
        out_specs=spec,
        out_shape=jax.ShapeDtypeStruct((XN * YN, LOCAL, 128), jnp.bfloat16),
        compiler_params=pltpu.CompilerParams(vmem_limit_bytes=VMEM),
        cost_estimate=pl.CostEstimate(flops=0, bytes_accessed=1 << 20, transcendentals=0),
        name="pick",
    )(z, *here(first, second))


def start_kernel(*refs):
    features, parts, total_ref, line = refs[:4], refs[4:10], refs[10], refs[11]
    depth = line.shape[1]
    tile = line.shape[2]
    for m in range(3):
        for step in range(QUART // tile):
            units = slice(step * tile, (step + 1) * tile)
            for route in range(2):
                x_ref = features[m // 2 * 2 + route]
                size = depth // 3
                for i, ref in enumerate(parts[3 * route : 3 * route + 3]):
                    line[route, i * size : (i + 1) * size] = ref[:, :, m, :, units].reshape(size, tile)
                for i in range(2):
                    rows = slice(i * ROWS, (i + 1) * ROWS)
                    total_ref[m, route, rows, units] = jnp.dot(
                        x_ref[rows, :depth], line[route], preferred_element_type=jnp.float32
                    )


def start(features, parts):
    outs = [((3, 2, 2 * ROWS, QUART), jnp.float32)]
    depth = TOKENS * 3 // 4
    scratch = [pltpu.VMEM((2, depth, QUART // 2), jnp.bfloat16)]
    return whole(start_kernel, "start", outs, (*features, *parts), 3 * 4 * ROWS * HALF * depth, scratch)[0]


def multiply_kernel(*refs):
    features, total_ref, parts = refs[:4], refs[4], refs[5:9]
    keep_ref, send_ref, rows_ref, cols_ref, line = refs[9:]
    depth = line.shape[1]
    tile = line.shape[2]
    for m in range(3):
        across = [jnp.zeros((ROWS, 128), jnp.float32) for _ in range(2)]
        for step in range(QUART // tile):
            units = slice(step * tile, (step + 1) * tile)
            for route in range(2):
                x_ref = features[m // 2 * 2 + route]
                size = depth // 2
                for i, ref in enumerate(parts[2 * route : 2 * route + 2]):
                    line[route, i * size : (i + 1) * size] = ref[:, :, m, :, units].reshape(size, tile)
                down = jnp.zeros((1, tile), jnp.float32)
                for i, out_ref in enumerate((keep_ref, send_ref)):
                    rows = slice(i * ROWS, (i + 1) * ROWS)
                    last = jnp.dot(x_ref[rows, TOKENS - depth :], line[route], preferred_element_type=jnp.float32)
                    grad = total_ref[m, route, rows, units] + last
                    out_ref[m, route, :, units] = grad.astype(jnp.bfloat16)
                    square = grad * grad
                    down += jnp.sum(square, axis=0, keepdims=True)
                    for k in range(tile // 128):
                        across[i] += square[:, k * 128 : (k + 1) * 128]
                for k in range(tile // 128):
                    row = step * (tile // 128) + k
                    row += (m * 2 + route) * 8
                    cols_ref[0, row : row + 1] = down[:, k * 128 : (k + 1) * 128] * SCALE
        for i, total in enumerate(across):
            rows_ref[i, m : m + 1] = jnp.sum(total.T, axis=0, keepdims=True) * SCALE
    for i in range(1, XN * YN):
        cols_ref[i] = cols_ref[0]


def multiply(features, total, parts):
    outs = [
        ((3, 2, ROWS, QUART), jnp.bfloat16),
        ((3, 2, ROWS, QUART), jnp.bfloat16),
        ((2, 3, ROWS), jnp.float32),
        ((XN * YN, 48, 128), jnp.float32),
    ]
    depth = TOKENS // 4
    scratch = [pltpu.VMEM((2, depth, QUART // 2), jnp.bfloat16)]
    return whole(multiply_kernel, "multiply", outs, (*features, total, *parts), 3 * 4 * ROWS * HALF * depth, scratch)


def span_kernel(parts_ref, old_ref, out_ref):
    total = parts_ref[0]
    for i in range(1, XN * YN):
        total += parts_ref[i]
    out_ref[...] = BETA * old_ref[...] + (1.0 - BETA) * (total * (1.0 / D) + EPS)


def weigh_kernel(rows_ref, mine_ref, other_ref, keep_ref, got_ref, out_ref):
    out_ref[0, 0:3] = rows_ref[...]
    for m in range(3):
        total = jnp.zeros((ROWS, 128), jnp.float32)
        for ref, span_ref in ((keep_ref, mine_ref), (got_ref, other_ref)):
            for route in range(2):
                at = (m * 2 + route) * 8
                inverse = 1.0 / span_ref[at : at + 8]
                for k in range(8):
                    grad = ref[m, route, :, k * 128 : (k + 1) * 128].astype(jnp.float32)
                    total += grad * grad * inverse[k : k + 1]
        out_ref[0, 3 + m : 4 + m] = jnp.sum(total.T, axis=0, keepdims=True) * SCALE
    for i in range(1, ZN):
        out_ref[i] = out_ref[0]


def width_kernel(parts_ref, old_ref, width_ref, out_ref):
    total = parts_ref[0]
    for i in range(1, ZN):
        total += parts_ref[i]
    width = BETA * old_ref[...] + (1.0 - BETA) * (total[0:3] * (1.0 / FF) + EPS)
    width_ref[...] = width
    squares = total[3:6] / width
    squares = squares[:, :128] + squares[:, 128:]
    for i in range(XN * YN * CN):
        out_ref[i] = squares


def finish_kernel(core_ref, parts_ref, width_ref, mine_ref, other_ref, keep_ref, got_ref, *refs):
    outs, widths, spans, bufs, sem = refs[:3], refs[3:6], refs[6:9], refs[9:12], refs[12]
    core = core_ref[0]
    squares = parts_ref[0]
    for i in range(1, XN * YN * CN):
        squares += parts_ref[i]
    rms = jnp.sqrt(jnp.sum(squares, axis=1, keepdims=True) * (1.0 / (D * FF)))
    scaled = lax.rsqrt(width_ref[...]) * ((1.0 / 32.0) / jnp.maximum(1.0, rms))
    copies = []
    for m in range(3):
        widths[m][...] = width_ref[m : m + 1]
        width = jnp.broadcast_to(scaled[m : m + 1], (128, ROWS)).T
        for ref, span_ref, at in ((keep_ref, mine_ref, core), (got_ref, other_ref, 1 - core)):
            spans[m][pl.ds(pl.multiple_of(at * 16, 16), 16)] = span_ref[m * 16 : (m + 1) * 16]
            for route in range(2):
                first = at * HALF + route * QUART
                row = (m * 2 + route) * 8
                unit = lax.rsqrt(span_ref[row : row + 8])
                for k in range(8):
                    grad = ref[m, route, :, k * 128 : (k + 1) * 128].astype(jnp.float32)
                    normed = (grad * width * unit[k : k + 1]).astype(jnp.bfloat16)
                    place = pl.ds(pl.multiple_of(first + k * 128, 128), 128)
                    if m < 2:
                        bufs[m][:, place] = normed
                    else:
                        bufs[m][place, :] = normed.T
                part = pl.ds(pl.multiple_of(first, QUART), QUART)
                ends = [v.at[:, part] if m < 2 else v.at[part] for v in (bufs[m], outs[m])]
                copies.append(pltpu.make_async_copy(*ends, sem.at[len(copies)]))
                copies[-1].start()
    for copy in copies:
        copy.wait()


def finish(core, *operands):
    spec = pl.BlockSpec(memory_space=pltpu.VMEM)
    steps = [(ROWS, COLS), (ROWS, COLS), (COLS, ROWS)]
    operands = here(*operands)
    return pl.pallas_call(
        finish_kernel,
        in_specs=[pl.BlockSpec(memory_space=pltpu.SMEM)] + [spec] * len(operands),
        out_specs=[pl.BlockSpec(memory_space=pl.ANY)] * 3 + [spec] * 6,
        out_shape=[jax.ShapeDtypeStruct(shape, jnp.bfloat16) for shape in steps]
        + [jax.ShapeDtypeStruct((1, ROWS), jnp.float32)] * 3
        + [jax.ShapeDtypeStruct((COLS // 128, 128), jnp.float32)] * 3,
        scratch_shapes=[pltpu.VMEM(shape, jnp.bfloat16) for shape in steps] + [pltpu.SemaphoreType.DMA((12,))],
        compiler_params=pltpu.CompilerParams(vmem_limit_bytes=2 * VMEM),
        cost_estimate=pl.CostEstimate(flops=12 * ROWS * COLS, bytes_accessed=12 << 20, transcendentals=0),
        name="finish",
    )(core, *operands)


def arrange_kernel(place_ref, mine_ref, other_ref, *outs):
    x, y, core = place_ref[0], place_ref[1], place_ref[2]
    for array in range(2):
        for part in range(4):
            column = array * 4 + lax.rem(core + part // 2, 2) * 2 + part % 2
            rows = slice(part * 128, (part + 1) * 128)
            for route in range(2):
                for outer in range(4):
                    blocks = []
                    for inner in range(4):
                        dx, dy = (ORDER[outer], ORDER[inner]) if route else (ORDER[inner], ORDER[outer])
                        source = lax.rem(x + dx, XN) * YN + lax.rem(y + dy, YN)
                        blocks += [mine_ref[column, source], other_ref[column, source]]
                    tokens = slice(outer * 256, (outer + 1) * 256)
                    outs[array * 2 + route][rows, tokens] = jnp.concatenate(blocks).T


def arrange(place, mine, other):
    spec = pl.BlockSpec(memory_space=pltpu.VMEM)
    return pl.pallas_call(
        arrange_kernel,
        in_specs=[pl.BlockSpec(memory_space=pltpu.SMEM), spec, spec],
        out_specs=[spec] * 4,
        out_shape=[pltpu.VMEM((2 * ROWS, TOKENS), jnp.bfloat16)] * 4,
        compiler_params=pltpu.CompilerParams(vmem_limit_bytes=VMEM),
        cost_estimate=pl.CostEstimate(flops=0, bytes_accessed=6 << 20, transcendentals=0),
        name="arrange",
    )(place, *here(mine, other))


def local(
    layer_input,
    output_grad,
    gate_pre,
    up_pre,
    hidden_grad,
    row_gate,
    col_gate,
    row_up,
    col_up,
    row_down,
    col_down,
):
    x, y, c, z = (lax.axis_index(name) for name in ("x", "y", "c", "z"))
    core = c.astype(jnp.int32).reshape(1)
    level = z.astype(jnp.int32).reshape(1)
    place = jnp.stack((x, y, c)).astype(jnp.int32)
    known = (core, level, place, c == 0, gate_pre, up_pre, hidden_grad)
    core, level, place, first, gate_pre, up_pre, hidden_grad = lax.optimization_barrier(known)
    old_span = jnp.stack((col_gate, col_up, row_down)).reshape(3, CN, 16, 128)
    old_span = jnp.where(first, old_span[:, 0], old_span[:, 1]).reshape(48, 128)
    old_width = jnp.stack((row_gate, row_up, col_down))

    def halves(at):
        return derive(*(lax.dynamic_slice_in_dim(v, at * HALF, HALF, 1) for v in (gate_pre, up_pre, hidden_grad)))

    got = swap(halves(1 - c))
    own = jnp.stack((halves(c), got))
    own_a, own_b = own[..., :QUART], own[..., QUART:]
    near = [neighbours(own_a, "x"), neighbours(own_b, "y")]

    chosen = pick(level, layer_input, output_grad)
    chosen = lax.all_to_all(chosen, ("x", "y"), split_axis=0, concat_axis=0, tiled=True)
    near, chosen, old_span, old_width = lax.optimization_barrier((near, chosen, old_span, old_width))
    far = relay(near, ("x", "y"))
    chosen = lax.all_gather(chosen, "z")
    lines = join([own_a, *near[0], *far[0], own_b, *near[1], *far[1]])

    near = [neighbours(line, axis) for line, axis in zip(lines, ("y", "x"))]
    far = relay(near, ("y", "x"))
    features = arrange(place, chosen, swap(chosen))
    parts = [lines[0], *near[0], lines[1], *near[1]]
    keep, send, rows, cols = multiply(features, start(features, parts), [*far[0], *far[1]])

    rows = rows[0] + swap(rows[1])
    rows, cols, send = lax.optimization_barrier((rows, cols, send))
    got = swap(send)

    parts = collect(cols, ("x", "y"))
    span = whole(span_kernel, "span", [((48, 128), jnp.float32)], (parts, old_span))[0]
    other = swap(span)
    sums = whole(weigh_kernel, "weigh", [((ZN, 6, ROWS), jnp.float32)], (rows, span, other, keep, got))[0]
    parts = collect(sums, ("z",))
    outs = [((3, ROWS), jnp.float32), ((XN * YN * CN, 3, 128), jnp.float32)]
    width, squares = whole(width_kernel, "width", outs, (parts, old_width))
    parts = collect(squares, ("x", "y", "c"))
    outs = finish(core, parts, width, span, other, keep, got)
    widths = [v.reshape(ROWS) for v in outs[3:6]]
    spans = [v.reshape(COLS) for v in outs[6:9]]
    return (*outs[:3], widths[0], spans[0], widths[1], spans[1], spans[2], widths[2])


def solution(mesh):
    grid = Mesh(mesh.devices.reshape(XN, YN, CN, ZN), ("x", "y", "c", "z"))
    dp = ("x", "y", "c")
    return jax.shard_map(
        local,
        mesh=grid,
        in_specs=(
            P(dp, None),
            P(dp, None),
            P(dp, "z"),
            P(dp, "z"),
            P(dp, "z"),
            P(dp),
            P("z"),
            P(dp),
            P("z"),
            P("z"),
            P(dp),
        ),
        out_specs=(
            P(dp, "z"),
            P(dp, "z"),
            P("z", dp),
            P(dp),
            P("z"),
            P(dp),
            P("z"),
            P("z"),
            P(dp),
        ),
        check_vma=False,
    )
```

```python
import jax
import jax.numpy as jnp
from jax import lax
from jax.experimental import pallas as pl
from jax.experimental.pallas import tpu as pltpu
from jax.sharding import Mesh, PartitionSpec as P

D = 8192
FF = 32768
STEP = 8
TOKENS = 1024

EPS = 1e-30
BETA = 1.0 - float(STEP) ** (-0.8)
XN, YN, CN, ZN = 4, 4, 2, 8
ROWS = D // (XN * YN * CN)
COLS = FF // ZN
HALF = COLS // 2
QUART = HALF // 2
LOCAL = TOKENS // (XN * YN * CN)
VMEM = 12 * 1024 * 1024
SCALE = 1.0 / TOKENS
ORDER = (0, 3, 1, 2)


def derive(gate_pre, up_pre, hidden_grad):
    first = gate_pre.astype(jnp.float32)
    second = up_pre.astype(jnp.float32)
    cotangent = hidden_grad.astype(jnp.float32)
    sigma = jax.nn.sigmoid(first)
    gate_cot = (cotangent * second * sigma * (1.0 + first * (1.0 - sigma))).astype(jnp.bfloat16)
    up_cot = (cotangent * first * sigma).astype(jnp.bfloat16)
    hidden = (first * sigma * second).astype(jnp.bfloat16)
    return jnp.stack((gate_cot, up_cot, hidden))


def shift(value, axis, size, step):
    return lax.ppermute(value, axis, [(i, (i + step) % size) for i in range(size)])


def swap(value):
    return shift(value, "c", CN, 1)


def neighbours(value, axis):
    return shift(value, axis, 4, 1), shift(value, axis, 4, 3)


def here(*values):
    return [pltpu.with_memory_space_constraint(v, pltpu.VMEM) for v in values]


def whole(kernel, name, outs, operands, flops=0, scratch=()):
    size = sum(v.size * v.dtype.itemsize for v in operands)
    spec = pl.BlockSpec(memory_space=pltpu.VMEM)
    return pl.pallas_call(
        kernel,
        in_specs=[spec] * len(operands),
        out_specs=[spec] * len(outs),
        out_shape=[pltpu.VMEM(shape, dtype) for shape, dtype in outs],
        scratch_shapes=list(scratch),
        compiler_params=pltpu.CompilerParams(vmem_limit_bytes=VMEM),
        cost_estimate=pl.CostEstimate(flops=flops, bytes_accessed=size, transcendentals=0),
        name=name,
    )(*here(*operands))


def halve_kernel(*refs):
    for i in range(4):
        half = refs[4 + i].shape[0]
        refs[4 + i][...] = refs[i][i % 2 * half : (i % 2 + 1) * half]


def relay(pairs, axes):
    arrived = [v for pair in pairs for v in pair]
    outs = [((v.shape[0] // 2,) + v.shape[1:], v.dtype) for v in arrived]
    halves = whole(halve_kernel, "halve", outs, arrived)
    return [(shift(halves[2 * r], axis, 4, 1), shift(halves[2 * r + 1], axis, 4, 3)) for r, axis in enumerate(axes)]


def collect(copies, axes):
    return lax.all_to_all(copies, axes, split_axis=0, concat_axis=0, tiled=True)


def join_kernel(*refs):
    for route in range(2):
        own, left, right, low, high = refs[5 * route : 5 * route + 5]
        line = refs[10 + route]
        for block, ref in enumerate((own, left, right)):
            line[block] = ref[...]
        line[3, 0] = low[0]
        line[3, 1] = high[0]


def join(blocks):
    return whole(join_kernel, "join", [((4, CN, 3, LOCAL, QUART), jnp.bfloat16)] * 2, blocks)


def pick_kernel(z_ref, first_ref, second_ref, out_ref, sem):
    for array, ref in enumerate((first_ref, second_ref)):

        @pl.when(lax.rem(z_ref[0], 2) == array)
        def _():
            copies = []
            for chip in range(XN * YN):
                start = pl.multiple_of((2 * chip + z_ref[0] // 2) * ROWS, ROWS)
                columns = ref.at[:, pl.ds(start, ROWS)]
                copies.append(pltpu.make_async_copy(columns, out_ref.at[chip], sem.at[chip]))
                copies[-1].start()
            for copy in copies:
                copy.wait()


def pick(z, first, second):
    return pl.pallas_call(
        pick_kernel,
        in_specs=[pl.BlockSpec(memory_space=pltpu.SMEM)] + [pl.BlockSpec(memory_space=pl.ANY)] * 2,
        out_specs=pl.BlockSpec(memory_space=pltpu.VMEM),
        out_shape=pltpu.VMEM((XN * YN, LOCAL, ROWS), jnp.bfloat16),
        scratch_shapes=[pltpu.SemaphoreType.DMA((XN * YN,))],
        compiler_params=pltpu.CompilerParams(vmem_limit_bytes=VMEM),
        cost_estimate=pl.CostEstimate(flops=0, bytes_accessed=1 << 20, transcendentals=0),
        name="pick",
    )(z, first, second)


def start_kernel(*refs):
    features, parts, total_ref, line = refs[:4], refs[4:10], refs[10], refs[11]
    depth = line.shape[1]
    tile = line.shape[2]
    for m in range(3):
        for step in range(QUART // tile):
            units = slice(step * tile, (step + 1) * tile)
            for route in range(2):
                x_ref = features[m // 2 * 2 + route]
                size = depth // 3
                for i, ref in enumerate(parts[3 * route : 3 * route + 3]):
                    line[route, i * size : (i + 1) * size] = ref[:, :, m, :, units].reshape(size, tile)
                for i in range(2):
                    rows = slice(i * ROWS, (i + 1) * ROWS)
                    total_ref[m, route, rows, units] = jnp.dot(
                        x_ref[rows, :depth], line[route], preferred_element_type=jnp.float32
                    )


def start(features, parts):
    outs = [((3, 2, 2 * ROWS, QUART), jnp.float32)]
    depth = TOKENS * 3 // 4
    scratch = [pltpu.VMEM((2, depth, QUART // 2), jnp.bfloat16)]
    return whole(start_kernel, "start", outs, (*features, *parts), 3 * 4 * ROWS * HALF * depth, scratch)[0]


def multiply_kernel(*refs):
    features, total_ref, parts = refs[:4], refs[4], refs[5:9]
    keep_ref, send_ref, rows_ref, cols_ref, line = refs[9:]
    depth = line.shape[1]
    tile = line.shape[2]
    for m in range(3):
        across = [jnp.zeros((ROWS, 128), jnp.float32) for _ in range(2)]
        for step in range(QUART // tile):
            units = slice(step * tile, (step + 1) * tile)
            for route in range(2):
                x_ref = features[m // 2 * 2 + route]
                size = depth // 2
                for i, ref in enumerate(parts[2 * route : 2 * route + 2]):
                    line[route, i * size : (i + 1) * size] = ref[:, :, m, :, units].reshape(size, tile)
                down = jnp.zeros((1, tile), jnp.float32)
                for i, out_ref in enumerate((keep_ref, send_ref)):
                    rows = slice(i * ROWS, (i + 1) * ROWS)
                    last = jnp.dot(x_ref[rows, TOKENS - depth :], line[route], preferred_element_type=jnp.float32)
                    grad = total_ref[m, route, rows, units] + last
                    out_ref[m, route, :, units] = grad.astype(jnp.bfloat16)
                    square = grad * grad
                    down += jnp.sum(square, axis=0, keepdims=True)
                    for k in range(tile // 128):
                        across[i] += square[:, k * 128 : (k + 1) * 128]
                for k in range(tile // 128):
                    row = step * (tile // 128) + k
                    row += (m * 2 + route) * 8
                    cols_ref[0, row : row + 1] = down[:, k * 128 : (k + 1) * 128] * SCALE
        for i, total in enumerate(across):
            rows_ref[i, m : m + 1] = jnp.sum(total.T, axis=0, keepdims=True) * SCALE
    for i in range(1, XN * YN):
        cols_ref[i] = cols_ref[0]


def multiply(features, total, parts):
    outs = [
        ((3, 2, ROWS, QUART), jnp.bfloat16),
        ((3, 2, ROWS, QUART), jnp.bfloat16),
        ((2, 3, ROWS), jnp.float32),
        ((XN * YN, 48, 128), jnp.float32),
    ]
    depth = TOKENS // 4
    scratch = [pltpu.VMEM((2, depth, QUART // 2), jnp.bfloat16)]
    return whole(multiply_kernel, "multiply", outs, (*features, total, *parts), 3 * 4 * ROWS * HALF * depth, scratch)


def span_kernel(parts_ref, old_ref, out_ref):
    total = parts_ref[0]
    for i in range(1, XN * YN):
        total += parts_ref[i]
    out_ref[...] = BETA * old_ref[...] + (1.0 - BETA) * (total * (1.0 / D) + EPS)


def weigh_kernel(rows_ref, met_ref, mine_ref, other_ref, keep_ref, got_ref, out_ref):
    out_ref[0, 0:3] = rows_ref[0] + met_ref[...]
    for m in range(3):
        total = jnp.zeros((ROWS, 128), jnp.float32)
        for ref, span_ref in ((keep_ref, mine_ref), (got_ref, other_ref)):
            for route in range(2):
                at = (m * 2 + route) * 8
                inverse = 1.0 / span_ref[at : at + 8]
                for k in range(8):
                    grad = ref[m, route, :, k * 128 : (k + 1) * 128].astype(jnp.float32)
                    total += grad * grad * inverse[k : k + 1]
        out_ref[0, 3 + m : 4 + m] = jnp.sum(total.T, axis=0, keepdims=True) * SCALE
    for i in range(1, ZN):
        out_ref[i] = out_ref[0]


def width_kernel(parts_ref, old_ref, width_ref, out_ref):
    total = parts_ref[0]
    for i in range(1, ZN):
        total += parts_ref[i]
    width = BETA * old_ref[...] + (1.0 - BETA) * (total[0:3] * (1.0 / FF) + EPS)
    width_ref[...] = width
    squares = total[3:6] / width
    squares = squares[:, :128] + squares[:, 128:]
    for i in range(XN * YN * CN):
        out_ref[i] = squares


def finish_kernel(core_ref, parts_ref, width_ref, mine_ref, other_ref, keep_ref, got_ref, *refs):
    outs, widths, spans, bufs, sem = refs[:3], refs[3:6], refs[6:9], refs[9:12], refs[12]
    core = core_ref[0]
    squares = parts_ref[0]
    for i in range(1, XN * YN * CN):
        squares += parts_ref[i]
    rms = jnp.sqrt(jnp.sum(squares, axis=1, keepdims=True) * (1.0 / (D * FF)))
    scaled = lax.rsqrt(width_ref[...]) * ((1.0 / 32.0) / jnp.maximum(1.0, rms))
    copies = []
    for m in range(3):
        widths[m][...] = width_ref[m : m + 1]
        width = jnp.broadcast_to(scaled[m : m + 1], (128, ROWS)).T
        for ref, span_ref, at in ((keep_ref, mine_ref, core), (got_ref, other_ref, 1 - core)):
            spans[m][pl.ds(pl.multiple_of(at * 16, 16), 16)] = span_ref[m * 16 : (m + 1) * 16]
            for route in range(2):
                first = at * HALF + route * QUART
                row = (m * 2 + route) * 8
                unit = lax.rsqrt(span_ref[row : row + 8])
                for k in range(8):
                    grad = ref[m, route, :, k * 128 : (k + 1) * 128].astype(jnp.float32)
                    normed = (grad * width * unit[k : k + 1]).astype(jnp.bfloat16)
                    place = pl.ds(pl.multiple_of(first + k * 128, 128), 128)
                    if m < 2:
                        bufs[m][:, place] = normed
                    else:
                        bufs[m][place, :] = normed.T
                part = pl.ds(pl.multiple_of(first, QUART), QUART)
                ends = [v.at[:, part] if m < 2 else v.at[part] for v in (bufs[m], outs[m])]
                copies.append(pltpu.make_async_copy(*ends, sem.at[len(copies)]))
                copies[-1].start()
    for copy in copies:
        copy.wait()


def finish(core, *operands):
    spec = pl.BlockSpec(memory_space=pltpu.VMEM)
    steps = [(ROWS, COLS), (ROWS, COLS), (COLS, ROWS)]
    operands = here(*operands)
    return pl.pallas_call(
        finish_kernel,
        in_specs=[pl.BlockSpec(memory_space=pltpu.SMEM)] + [spec] * len(operands),
        out_specs=[pl.BlockSpec(memory_space=pl.ANY)] * 3 + [spec] * 6,
        out_shape=[jax.ShapeDtypeStruct(shape, jnp.bfloat16) for shape in steps]
        + [jax.ShapeDtypeStruct((1, ROWS), jnp.float32)] * 3
        + [jax.ShapeDtypeStruct((COLS // 128, 128), jnp.float32)] * 3,
        scratch_shapes=[pltpu.VMEM(shape, jnp.bfloat16) for shape in steps] + [pltpu.SemaphoreType.DMA((12,))],
        compiler_params=pltpu.CompilerParams(vmem_limit_bytes=2 * VMEM),
        cost_estimate=pl.CostEstimate(flops=12 * ROWS * COLS, bytes_accessed=12 << 20, transcendentals=0),
        name="finish",
    )(core, *operands)


def arrange_kernel(place_ref, *refs):
    x, y, core, quarter = (place_ref[i] for i in range(4))
    sources, outs = refs[:4], refs[4:]
    for array in range(2):
        for part in range(4):
            slot = lax.rem(core + part // 2 + quarter // 2, 2)
            columns = slice(part % 2 * 128, (part % 2 + 1) * 128)
            rows = slice(part * 128, (part + 1) * 128)
            for route in range(2):
                for outer in range(4):
                    blocks = []
                    for inner in range(4):
                        dx, dy = (ORDER[outer], ORDER[inner]) if route else (ORDER[inner], ORDER[outer])
                        chip = lax.rem(x + dx, XN) * YN + lax.rem(y + dy, YN)
                        for own, met in (sources[:2], sources[2:]):
                            mine, theirs = (ref[slot, chip, :, columns] for ref in (own, met))
                            blocks.append(jnp.where(lax.rem(quarter, 2) == array, mine, theirs))
                    tokens = slice(outer * 256, (outer + 1) * 256)
                    outs[array * 2 + route][rows, tokens] = jnp.concatenate(blocks).T


def arrange(place, *sources):
    spec = pl.BlockSpec(memory_space=pltpu.VMEM)
    return pl.pallas_call(
        arrange_kernel,
        in_specs=[pl.BlockSpec(memory_space=pltpu.SMEM)] + [spec] * 4,
        out_specs=[spec] * 4,
        out_shape=[pltpu.VMEM((2 * ROWS, TOKENS), jnp.bfloat16)] * 4,
        compiler_params=pltpu.CompilerParams(vmem_limit_bytes=VMEM),
        cost_estimate=pl.CostEstimate(flops=0, bytes_accessed=6 << 20, transcendentals=0),
        name="arrange",
    )(place, *here(*sources))


def local(
    layer_input,
    output_grad,
    gate_pre,
    up_pre,
    hidden_grad,
    row_gate,
    col_gate,
    row_up,
    col_up,
    row_down,
    col_down,
):
    x, y, c, z = (lax.axis_index(name) for name in ("x", "y", "c", "z"))
    core = c.astype(jnp.int32).reshape(1)
    quarter = lax.rem(z, 4).astype(jnp.int32).reshape(1)
    place = jnp.stack((x, y, c, lax.rem(z, 4))).astype(jnp.int32)
    known = (core, quarter, place, c == 0, gate_pre, up_pre, hidden_grad)
    core, quarter, place, first, gate_pre, up_pre, hidden_grad = lax.optimization_barrier(known)
    old_span = jnp.stack((col_gate, col_up, row_down)).reshape(3, CN, 16, 128)
    old_span = jnp.where(first, old_span[:, 0], old_span[:, 1]).reshape(48, 128)
    old_width = jnp.stack((row_gate, row_up, col_down))

    def halves(at):
        return derive(*(lax.dynamic_slice_in_dim(v, at * HALF, HALF, 1) for v in (gate_pre, up_pre, hidden_grad)))

    got = swap(halves(1 - c))
    own = jnp.stack((halves(c), got))
    own_a, own_b = own[..., :QUART], own[..., QUART:]
    near = [neighbours(own_a, "x"), neighbours(own_b, "y")]

    chosen = pick(quarter, layer_input, output_grad)
    chosen = lax.all_to_all(chosen, ("x", "y"), split_axis=0, concat_axis=0, tiled=True)
    near, chosen, old_span, old_width = lax.optimization_barrier((near, chosen, old_span, old_width))
    far = relay(near, ("x", "y"))
    lines = join([own_a, *near[0], *far[0], own_b, *near[1], *far[1]])

    near = [neighbours(line, axis) for line, axis in zip(lines, ("y", "x"))]
    far = relay(near, ("y", "x"))
    chosen = jnp.stack((chosen, lax.ppermute(chosen, "z", [(i, i ^ 2) for i in range(ZN)])))
    met = lax.ppermute(chosen, "z", [(i, i ^ 1) for i in range(ZN)])
    features = arrange(place, chosen, met, swap(chosen), swap(met))
    parts = [lines[0], *near[0], lines[1], *near[1]]
    keep, send, rows, cols = multiply(features, start(features, parts), [*far[0], *far[1]])

    met = swap(rows[1])
    got = swap(send)

    parts = collect(cols, ("x", "y"))
    span = whole(span_kernel, "span", [((48, 128), jnp.float32)], (parts, old_span))[0]
    other = swap(span)
    sums = whole(weigh_kernel, "weigh", [((ZN, 6, ROWS), jnp.float32)], (rows, met, span, other, keep, got))[0]
    parts = collect(sums, ("z",))
    outs = [((3, ROWS), jnp.float32), ((XN * YN * CN, 3, 128), jnp.float32)]
    width, squares = whole(width_kernel, "width", outs, (parts, old_width))
    parts = collect(squares, ("x", "y", "c"))
    outs = finish(core, parts, width, span, other, keep, got)
    widths = [v.reshape(ROWS) for v in outs[3:6]]
    spans = [v.reshape(COLS) for v in outs[6:9]]
    return (*outs[:3], widths[0], spans[0], widths[1], spans[1], spans[2], widths[2])


def solution(mesh):
    grid = Mesh(mesh.devices.reshape(XN, YN, CN, ZN), ("x", "y", "c", "z"))
    dp = ("x", "y", "c")
    return jax.shard_map(
        local,
        mesh=grid,
        in_specs=(
            P(dp, None),
            P(dp, None),
            P(dp, "z"),
            P(dp, "z"),
            P(dp, "z"),
            P(dp),
            P("z"),
            P(dp),
            P("z"),
            P("z"),
            P(dp),
        ),
        out_specs=(
            P(dp, "z"),
            P(dp, "z"),
            P("z", dp),
            P(dp),
            P("z"),
            P(dp),
            P("z"),
            P("z"),
            P(dp),
        ),
        check_vma=False,
    )
```

```python
import jax
import jax.numpy as jnp
from jax import lax
from jax.experimental import pallas as pl
from jax.experimental.pallas import tpu as pltpu
from jax.sharding import Mesh, PartitionSpec as P

D = 8192
FF = 32768
STEP = 8
TOKENS = 1024

EPS = 1e-30
BETA = 1.0 - float(STEP) ** (-0.8)
XN, YN, CN, ZN = 4, 4, 2, 8
ROWS = D // (XN * YN * CN)
COLS = FF // ZN
HALF = COLS // 2
QUART = HALF // 2
LOCAL = TOKENS // (XN * YN * CN)
VMEM = 12 * 1024 * 1024
SCALE = 1.0 / TOKENS
ORDER = (0, 3, 1, 2)


def derive(gate_pre, up_pre, hidden_grad):
    first = gate_pre.astype(jnp.float32)
    second = up_pre.astype(jnp.float32)
    cotangent = hidden_grad.astype(jnp.float32)
    sigma = jax.nn.sigmoid(first)
    gate_cot = (cotangent * second * sigma * (1.0 + first * (1.0 - sigma))).astype(jnp.bfloat16)
    up_cot = (cotangent * first * sigma).astype(jnp.bfloat16)
    hidden = (first * sigma * second).astype(jnp.bfloat16)
    return jnp.stack((gate_cot, up_cot, hidden))


def shift(value, axis, size, step):
    return lax.ppermute(value, axis, [(i, (i + step) % size) for i in range(size)])


def swap(value):
    return shift(value, "c", CN, 1)


def neighbours(value, axis):
    return shift(value, axis, 4, 1), shift(value, axis, 4, 3)


def here(*values):
    return [pltpu.with_memory_space_constraint(v, pltpu.VMEM) for v in values]


def whole(kernel, name, outs, operands, flops=0, scratch=()):
    size = sum(v.size * v.dtype.itemsize for v in operands)
    spec = pl.BlockSpec(memory_space=pltpu.VMEM)
    return pl.pallas_call(
        kernel,
        in_specs=[spec] * len(operands),
        out_specs=[spec] * len(outs),
        out_shape=[pltpu.VMEM(shape, dtype) for shape, dtype in outs],
        scratch_shapes=list(scratch),
        compiler_params=pltpu.CompilerParams(vmem_limit_bytes=VMEM),
        cost_estimate=pl.CostEstimate(flops=flops, bytes_accessed=size, transcendentals=0),
        name=name,
    )(*here(*operands))


def halve_kernel(*refs):
    for i in range(4):
        half = refs[4 + i].shape[0]
        refs[4 + i][...] = refs[i][i % 2 * half : (i % 2 + 1) * half]


def relay(pairs, axes):
    arrived = [v for pair in pairs for v in pair]
    outs = [((v.shape[0] // 2,) + v.shape[1:], v.dtype) for v in arrived]
    halves = whole(halve_kernel, "halve", outs, arrived)
    return [(shift(halves[2 * r], axis, 4, 1), shift(halves[2 * r + 1], axis, 4, 3)) for r, axis in enumerate(axes)]


def collect(copies, axes):
    return lax.all_to_all(copies, axes, split_axis=0, concat_axis=0, tiled=True)


def join_kernel(*refs):
    for route in range(2):
        own, left, right, low, high = refs[5 * route : 5 * route + 5]
        line = refs[10 + route]
        for block, ref in enumerate((own, left, right)):
            line[block] = ref[...]
        line[3, 0] = low[0]
        line[3, 1] = high[0]


def join(blocks):
    return whole(join_kernel, "join", [((4, CN, 3, LOCAL, QUART), jnp.bfloat16)] * 2, blocks)


def pick_kernel(z_ref, first_ref, second_ref, out_ref, sem):
    for array, ref in enumerate((first_ref, second_ref)):

        @pl.when(lax.rem(z_ref[0], 2) == array)
        def _():
            copies = []
            for chip in range(XN * YN):
                start = pl.multiple_of((2 * chip + z_ref[0] // 2) * ROWS, ROWS)
                columns = ref.at[:, pl.ds(start, ROWS)]
                copies.append(pltpu.make_async_copy(columns, out_ref.at[chip], sem.at[chip]))
                copies[-1].start()
            for copy in copies:
                copy.wait()


def pick(z, first, second):
    return pl.pallas_call(
        pick_kernel,
        in_specs=[pl.BlockSpec(memory_space=pltpu.SMEM)] + [pl.BlockSpec(memory_space=pl.ANY)] * 2,
        out_specs=pl.BlockSpec(memory_space=pltpu.VMEM),
        out_shape=pltpu.VMEM((XN * YN, LOCAL, ROWS), jnp.bfloat16),
        scratch_shapes=[pltpu.SemaphoreType.DMA((XN * YN,))],
        compiler_params=pltpu.CompilerParams(vmem_limit_bytes=VMEM),
        cost_estimate=pl.CostEstimate(flops=0, bytes_accessed=1 << 20, transcendentals=0),
        name="pick",
    )(z, first, second)


def start_kernel(*refs):
    features, parts, total_ref, line = refs[:4], refs[4:10], refs[10], refs[11]
    depth = line.shape[1]
    tile = line.shape[2]
    for m in range(3):
        for step in range(QUART // tile):
            units = slice(step * tile, (step + 1) * tile)
            for route in range(2):
                x_ref = features[m // 2 * 2 + route]
                size = depth // 3
                for i, ref in enumerate(parts[3 * route : 3 * route + 3]):
                    line[route, i * size : (i + 1) * size] = ref[:, :, m, :, units].reshape(size, tile)
                for i in range(2):
                    rows = slice(i * ROWS, (i + 1) * ROWS)
                    total_ref[m, route, rows, units] = jnp.dot(
                        x_ref[rows, :depth], line[route], preferred_element_type=jnp.float32
                    )


def start(features, parts):
    outs = [((3, 2, 2 * ROWS, QUART), jnp.float32)]
    depth = TOKENS * 3 // 4
    scratch = [pltpu.VMEM((2, depth, QUART // 2), jnp.bfloat16)]
    return whole(start_kernel, "start", outs, (*features, *parts), 3 * 4 * ROWS * HALF * depth, scratch)[0]


def multiply_kernel(*refs):
    features, total_ref, parts = refs[:4], refs[4], refs[5:9]
    keep_ref, send_ref, rows_ref, cols_ref, line = refs[9:]
    depth = line.shape[1]
    tile = line.shape[2]
    for m in range(3):
        across = [jnp.zeros((ROWS, 128), jnp.float32) for _ in range(2)]
        for step in range(QUART // tile):
            units = slice(step * tile, (step + 1) * tile)
            for route in range(2):
                x_ref = features[m // 2 * 2 + route]
                size = depth // 2
                for i, ref in enumerate(parts[2 * route : 2 * route + 2]):
                    line[route, i * size : (i + 1) * size] = ref[:, :, m, :, units].reshape(size, tile)
                down = jnp.zeros((1, tile), jnp.float32)
                for i, out_ref in enumerate((keep_ref, send_ref)):
                    rows = slice(i * ROWS, (i + 1) * ROWS)
                    last = jnp.dot(x_ref[rows, TOKENS - depth :], line[route], preferred_element_type=jnp.float32)
                    grad = total_ref[m, route, rows, units] + last
                    out_ref[m, route, :, units] = grad.astype(jnp.bfloat16)
                    square = grad * grad
                    down += jnp.sum(square, axis=0, keepdims=True)
                    for k in range(tile // 128):
                        across[i] += square[:, k * 128 : (k + 1) * 128]
                for k in range(tile // 128):
                    row = step * (tile // 128) + k
                    row += (m * 2 + route) * 8
                    cols_ref[0, row : row + 1] = down[:, k * 128 : (k + 1) * 128] * SCALE
        for i, total in enumerate(across):
            rows_ref[i, m : m + 1] = jnp.sum(total.T, axis=0, keepdims=True) * SCALE
    for i in range(1, XN * YN):
        cols_ref[i] = cols_ref[0]


def multiply(features, total, parts):
    outs = [
        ((3, 2, ROWS, QUART), jnp.bfloat16),
        ((3, 2, ROWS, QUART), jnp.bfloat16),
        ((2, 3, ROWS), jnp.float32),
        ((XN * YN, 48, 128), jnp.float32),
    ]
    depth = TOKENS // 4
    scratch = [pltpu.VMEM((2, depth, QUART // 2), jnp.bfloat16)]
    return whole(multiply_kernel, "multiply", outs, (*features, total, *parts), 3 * 4 * ROWS * HALF * depth, scratch)


def span_kernel(parts_ref, old_ref, out_ref):
    total = parts_ref[0]
    for i in range(1, XN * YN):
        total += parts_ref[i]
    out_ref[...] = BETA * old_ref[...] + (1.0 - BETA) * (total * (1.0 / D) + EPS)


def weigh_kernel(rows_ref, met_ref, mine_ref, other_ref, keep_ref, got_ref, out_ref):
    out_ref[0, 0:3] = rows_ref[0] + met_ref[...]
    for m in range(3):
        total = jnp.zeros((ROWS, 128), jnp.float32)
        for ref, span_ref in ((keep_ref, mine_ref), (got_ref, other_ref)):
            for route in range(2):
                at = (m * 2 + route) * 8
                inverse = 1.0 / span_ref[at : at + 8]
                for k in range(8):
                    grad = ref[m, route, :, k * 128 : (k + 1) * 128].astype(jnp.float32)
                    total += grad * grad * inverse[k : k + 1]
        out_ref[0, 3 + m : 4 + m] = jnp.sum(total.T, axis=0, keepdims=True) * SCALE
    for i in range(1, ZN):
        out_ref[i] = out_ref[0]


def width_kernel(parts_ref, old_ref, width_ref, out_ref):
    total = parts_ref[0]
    for i in range(1, ZN):
        total += parts_ref[i]
    width = BETA * old_ref[...] + (1.0 - BETA) * (total[0:3] * (1.0 / FF) + EPS)
    width_ref[...] = width
    squares = total[3:6] / width
    squares = squares[:, :128] + squares[:, 128:]
    for i in range(XN * YN * CN):
        out_ref[i] = squares


def finish_kernel(core_ref, parts_ref, width_ref, mine_ref, other_ref, keep_ref, got_ref, *refs):
    outs, widths, spans, bufs, sem = refs[:3], refs[3:6], refs[6:9], refs[9:12], refs[12]
    core = core_ref[0]
    squares = parts_ref[0]
    for i in range(1, XN * YN * CN):
        squares += parts_ref[i]
    rms = jnp.sqrt(jnp.sum(squares, axis=1, keepdims=True) * (1.0 / (D * FF)))
    scaled = lax.rsqrt(width_ref[...]) * ((1.0 / 32.0) / jnp.maximum(1.0, rms))
    copies = []
    for m in range(3):
        widths[m][...] = width_ref[m : m + 1]
        width = jnp.broadcast_to(scaled[m : m + 1], (128, ROWS)).T
        for ref, span_ref, at in ((keep_ref, mine_ref, core), (got_ref, other_ref, 1 - core)):
            spans[m][pl.ds(pl.multiple_of(at * 16, 16), 16)] = span_ref[m * 16 : (m + 1) * 16]
            for route in range(2):
                first = at * HALF + route * QUART
                row = (m * 2 + route) * 8
                unit = lax.rsqrt(span_ref[row : row + 8])
                for k in range(8):
                    grad = ref[m, route, :, k * 128 : (k + 1) * 128].astype(jnp.float32)
                    normed = (grad * width * unit[k : k + 1]).astype(jnp.bfloat16)
                    place = pl.ds(pl.multiple_of(first + k * 128, 128), 128)
                    if m < 2:
                        bufs[m][:, place] = normed
                    else:
                        bufs[m][place, :] = normed.T
                part = pl.ds(pl.multiple_of(first, QUART), QUART)
                ends = [v.at[:, part] if m < 2 else v.at[part] for v in (bufs[m], outs[m])]
                copies.append(pltpu.make_async_copy(*ends, sem.at[len(copies)]))
                copies[-1].start()
    for copy in copies:
        copy.wait()


def finish(core, *operands):
    spec = pl.BlockSpec(memory_space=pltpu.VMEM)
    steps = [(ROWS, COLS), (ROWS, COLS), (COLS, ROWS)]
    operands = here(*operands)
    return pl.pallas_call(
        finish_kernel,
        in_specs=[pl.BlockSpec(memory_space=pltpu.SMEM)] + [spec] * len(operands),
        out_specs=[pl.BlockSpec(memory_space=pl.ANY)] * 3 + [spec] * 6,
        out_shape=[jax.ShapeDtypeStruct(shape, jnp.bfloat16) for shape in steps]
        + [jax.ShapeDtypeStruct((1, ROWS), jnp.float32)] * 3
        + [jax.ShapeDtypeStruct((COLS // 128, 128), jnp.float32)] * 3,
        scratch_shapes=[pltpu.VMEM(shape, jnp.bfloat16) for shape in steps] + [pltpu.SemaphoreType.DMA((12,))],
        compiler_params=pltpu.CompilerParams(vmem_limit_bytes=2 * VMEM),
        cost_estimate=pl.CostEstimate(flops=12 * ROWS * COLS, bytes_accessed=12 << 20, transcendentals=0),
        name="finish",
    )(core, *operands)


def arrange_kernel(place_ref, *refs):
    x, y, core, quarter = (place_ref[i] for i in range(4))
    sources, outs = refs[:4], refs[4:]
    for array in range(2):
        for part in range(4):
            slot = lax.rem(core + part // 2 + quarter // 2, 2)
            columns = slice(part % 2 * 128, (part % 2 + 1) * 128)
            rows = slice(part * 128, (part + 1) * 128)
            for route in range(2):
                for outer in range(4):
                    blocks = []
                    for inner in range(4):
                        dx, dy = (ORDER[outer], ORDER[inner]) if route else (ORDER[inner], ORDER[outer])
                        chip = lax.rem(x + dx, XN) * YN + lax.rem(y + dy, YN)
                        for own, met in (sources[:2], sources[2:]):
                            mine, theirs = (ref[slot, chip, :, columns] for ref in (own, met))
                            blocks.append(jnp.where(lax.rem(quarter, 2) == array, mine, theirs))
                    tokens = slice(outer * 256, (outer + 1) * 256)
                    outs[array * 2 + route][rows, tokens] = jnp.concatenate(blocks).T


def arrange(place, *sources):
    spec = pl.BlockSpec(memory_space=pltpu.VMEM)
    return pl.pallas_call(
        arrange_kernel,
        in_specs=[pl.BlockSpec(memory_space=pltpu.SMEM)] + [spec] * 4,
        out_specs=[spec] * 4,
        out_shape=[pltpu.VMEM((2 * ROWS, TOKENS), jnp.bfloat16)] * 4,
        compiler_params=pltpu.CompilerParams(vmem_limit_bytes=VMEM),
        cost_estimate=pl.CostEstimate(flops=0, bytes_accessed=6 << 20, transcendentals=0),
        name="arrange",
    )(place, *here(*sources))


def local(
    layer_input,
    output_grad,
    gate_pre,
    up_pre,
    hidden_grad,
    row_gate,
    col_gate,
    row_up,
    col_up,
    row_down,
    col_down,
):
    x, y, c, z = (lax.axis_index(name) for name in ("x", "y", "c", "z"))
    core = c.astype(jnp.int32).reshape(1)
    quarter = lax.rem(z, 4).astype(jnp.int32).reshape(1)
    place = jnp.stack((x, y, c, lax.rem(z, 4))).astype(jnp.int32)
    known = (core, quarter, place, c == 0, gate_pre, up_pre, hidden_grad)
    core, quarter, place, first, gate_pre, up_pre, hidden_grad = lax.optimization_barrier(known)
    old_span = jnp.stack((col_gate, col_up, row_down)).reshape(3, CN, 16, 128)
    old_span = jnp.where(first, old_span[:, 0], old_span[:, 1]).reshape(48, 128)
    old_width = jnp.stack((row_gate, row_up, col_down))

    def halves(at):
        return derive(*(lax.dynamic_slice_in_dim(v, at * HALF, HALF, 1) for v in (gate_pre, up_pre, hidden_grad)))

    got = swap(halves(1 - c))
    own = jnp.stack((halves(c), got))
    own_a, own_b = own[..., :QUART], own[..., QUART:]
    chosen = pick(quarter, layer_input, output_grad)
    own_a, own_b, chosen = lax.optimization_barrier((own_a, own_b, chosen))
    near = [neighbours(own_a, "x"), neighbours(own_b, "y")]
    chosen = lax.all_to_all(chosen, ("x", "y"), split_axis=0, concat_axis=0, tiled=True)
    near, chosen, old_span, old_width = lax.optimization_barrier((near, chosen, old_span, old_width))
    far = relay(near, ("x", "y"))
    lines = join([own_a, *near[0], *far[0], own_b, *near[1], *far[1]])

    near = [neighbours(line, axis) for line, axis in zip(lines, ("y", "x"))]
    far = relay(near, ("y", "x"))
    chosen = jnp.stack((chosen, lax.ppermute(chosen, "z", [(i, i ^ 2) for i in range(ZN)])))
    met = lax.ppermute(chosen, "z", [(i, i ^ 1) for i in range(ZN)])
    features = arrange(place, chosen, met, swap(chosen), swap(met))
    parts = [lines[0], *near[0], lines[1], *near[1]]
    keep, send, rows, cols = multiply(features, start(features, parts), [*far[0], *far[1]])

    met = swap(rows[1])
    got = swap(send)

    parts = collect(cols, ("x", "y"))
    span = whole(span_kernel, "span", [((48, 128), jnp.float32)], (parts, old_span))[0]
    other = swap(span)
    sums = whole(weigh_kernel, "weigh", [((ZN, 6, ROWS), jnp.float32)], (rows, met, span, other, keep, got))[0]
    parts = collect(sums, ("z",))
    outs = [((3, ROWS), jnp.float32), ((XN * YN * CN, 3, 128), jnp.float32)]
    width, squares = whole(width_kernel, "width", outs, (parts, old_width))
    parts = collect(squares, ("x", "y", "c"))
    outs = finish(core, parts, width, span, other, keep, got)
    widths = [v.reshape(ROWS) for v in outs[3:6]]
    spans = [v.reshape(COLS) for v in outs[6:9]]
    return (*outs[:3], widths[0], spans[0], widths[1], spans[1], spans[2], widths[2])


def solution(mesh):
    grid = Mesh(mesh.devices.reshape(XN, YN, CN, ZN), ("x", "y", "c", "z"))
    dp = ("x", "y", "c")
    return jax.shard_map(
        local,
        mesh=grid,
        in_specs=(
            P(dp, None),
            P(dp, None),
            P(dp, "z"),
            P(dp, "z"),
            P(dp, "z"),
            P(dp),
            P("z"),
            P(dp),
            P("z"),
            P("z"),
            P(dp),
        ),
        out_specs=(
            P(dp, "z"),
            P(dp, "z"),
            P("z", dp),
            P(dp),
            P("z"),
            P(dp),
            P("z"),
            P("z"),
            P(dp),
        ),
        check_vma=False,
    )
```

```python
import jax
import jax.numpy as jnp
from jax import lax
from jax.experimental import pallas as pl
from jax.experimental.pallas import tpu as pltpu
from jax.sharding import Mesh, PartitionSpec as P

D = 8192
FF = 32768
STEP = 8
TOKENS = 1024

EPS = 1e-30
BETA = 1.0 - float(STEP) ** (-0.8)
XN, YN, CN, ZN = 4, 4, 2, 8
ROWS = D // (XN * YN * CN)
COLS = FF // ZN
HALF = COLS // 2
QUART = HALF // 2
LOCAL = TOKENS // (XN * YN * CN)
VMEM = 12 * 1024 * 1024
SCALE = 1.0 / TOKENS
ORDER = (0, 3, 1, 2)


def derive(gate_pre, up_pre, hidden_grad):
    first = gate_pre.astype(jnp.float32)
    second = up_pre.astype(jnp.float32)
    cotangent = hidden_grad.astype(jnp.float32)
    sigma = jax.nn.sigmoid(first)
    gate_cot = (cotangent * second * sigma * (1.0 + first * (1.0 - sigma))).astype(jnp.bfloat16)
    up_cot = (cotangent * first * sigma).astype(jnp.bfloat16)
    hidden = (first * sigma * second).astype(jnp.bfloat16)
    return jnp.stack((gate_cot, up_cot, hidden))


def shift(value, axis, size, step):
    return lax.ppermute(value, axis, [(i, (i + step) % size) for i in range(size)])


def swap(value):
    return shift(value, "c", CN, 1)


def neighbours(value, axis):
    return shift(value, axis, 4, 1), shift(value, axis, 4, 3)


def here(*values):
    return [pltpu.with_memory_space_constraint(v, pltpu.VMEM) for v in values]


def whole(kernel, name, outs, operands, flops=0, scratch=()):
    size = sum(v.size * v.dtype.itemsize for v in operands)
    spec = pl.BlockSpec(memory_space=pltpu.VMEM)
    return pl.pallas_call(
        kernel,
        in_specs=[spec] * len(operands),
        out_specs=[spec] * len(outs),
        out_shape=[pltpu.VMEM(shape, dtype) for shape, dtype in outs],
        scratch_shapes=list(scratch),
        compiler_params=pltpu.CompilerParams(vmem_limit_bytes=VMEM),
        cost_estimate=pl.CostEstimate(flops=flops, bytes_accessed=size, transcendentals=0),
        name=name,
    )(*here(*operands))


def halve_kernel(*refs):
    for i in range(4):
        half = refs[4 + i].shape[0]
        refs[4 + i][...] = refs[i][i % 2 * half : (i % 2 + 1) * half]


def relay(pairs, axes):
    arrived = [v for pair in pairs for v in pair]
    outs = [((v.shape[0] // 2,) + v.shape[1:], v.dtype) for v in arrived]
    halves = whole(halve_kernel, "halve", outs, arrived)
    return [(shift(halves[2 * r], axis, 4, 1), shift(halves[2 * r + 1], axis, 4, 3)) for r, axis in enumerate(axes)]


def collect(copies, axes):
    return lax.all_to_all(copies, axes, split_axis=0, concat_axis=0, tiled=True)


def join_kernel(*refs):
    for route in range(2):
        own, left, right, low, high = refs[5 * route : 5 * route + 5]
        line = refs[10 + route]
        for block, ref in enumerate((own, left, right)):
            line[block] = ref[...]
        line[3, 0] = low[0]
        line[3, 1] = high[0]


def join(blocks):
    return whole(join_kernel, "join", [((4, CN, 3, LOCAL, QUART), jnp.bfloat16)] * 2, blocks)


def pick_kernel(z_ref, first_ref, second_ref, out_ref, sem):
    for array, ref in enumerate((first_ref, second_ref)):

        @pl.when(lax.rem(z_ref[0], 2) == array)
        def _():
            copies = []
            for chip in range(XN * YN):
                start = pl.multiple_of((2 * chip + z_ref[0] // 2) * ROWS, ROWS)
                columns = ref.at[:, pl.ds(start, ROWS)]
                copies.append(pltpu.make_async_copy(columns, out_ref.at[chip], sem.at[chip]))
                copies[-1].start()
            for copy in copies:
                copy.wait()


def pick(z, first, second):
    return pl.pallas_call(
        pick_kernel,
        in_specs=[pl.BlockSpec(memory_space=pltpu.SMEM)] + [pl.BlockSpec(memory_space=pl.ANY)] * 2,
        out_specs=pl.BlockSpec(memory_space=pltpu.VMEM),
        out_shape=pltpu.VMEM((XN * YN, LOCAL, ROWS), jnp.bfloat16),
        scratch_shapes=[pltpu.SemaphoreType.DMA((XN * YN,))],
        compiler_params=pltpu.CompilerParams(vmem_limit_bytes=VMEM),
        cost_estimate=pl.CostEstimate(flops=0, bytes_accessed=1 << 20, transcendentals=0),
        name="pick",
    )(z, first, second)


def start_kernel(*refs):
    features, parts, total_ref, line = refs[:4], refs[4:10], refs[10], refs[11]
    depth = line.shape[1]
    tile = line.shape[2]
    for m in range(3):
        for step in range(QUART // tile):
            units = slice(step * tile, (step + 1) * tile)
            for route in range(2):
                x_ref = features[m // 2 * 2 + route]
                size = depth // 3
                for i, ref in enumerate(parts[3 * route : 3 * route + 3]):
                    line[route, i * size : (i + 1) * size] = ref[:, :, m, :, units].reshape(size, tile)
                for i in range(2):
                    rows = slice(i * ROWS, (i + 1) * ROWS)
                    total_ref[m, route, rows, units] = jnp.dot(
                        x_ref[rows, :depth], line[route], preferred_element_type=jnp.float32
                    )


def start(features, parts):
    outs = [((3, 2, 2 * ROWS, QUART), jnp.float32)]
    depth = TOKENS * 3 // 4
    scratch = [pltpu.VMEM((2, depth, QUART // 2), jnp.bfloat16)]
    return whole(start_kernel, "start", outs, (*features, *parts), 3 * 4 * ROWS * HALF * depth, scratch)[0]


def multiply_kernel(*refs):
    features, total_ref, parts = refs[:4], refs[4], refs[5:9]
    keep_ref, send_ref, rows_ref, cols_ref, line = refs[9:]
    depth = line.shape[1]
    tile = line.shape[2]
    for m in range(3):
        across = [jnp.zeros((ROWS, 128), jnp.float32) for _ in range(2)]
        for step in range(QUART // tile):
            units = slice(step * tile, (step + 1) * tile)
            for route in range(2):
                x_ref = features[m // 2 * 2 + route]
                size = depth // 2
                for i, ref in enumerate(parts[2 * route : 2 * route + 2]):
                    line[route, i * size : (i + 1) * size] = ref[:, :, m, :, units].reshape(size, tile)
                down = jnp.zeros((1, tile), jnp.float32)
                for i, out_ref in enumerate((keep_ref, send_ref)):
                    rows = slice(i * ROWS, (i + 1) * ROWS)
                    last = jnp.dot(x_ref[rows, TOKENS - depth :], line[route], preferred_element_type=jnp.float32)
                    grad = total_ref[m, route, rows, units] + last
                    out_ref[m, route, :, units] = grad.astype(jnp.bfloat16)
                    square = grad * grad
                    down += jnp.sum(square, axis=0, keepdims=True)
                    for k in range(tile // 128):
                        across[i] += square[:, k * 128 : (k + 1) * 128]
                for k in range(tile // 128):
                    row = step * (tile // 128) + k
                    row += (m * 2 + route) * 8
                    cols_ref[0, row : row + 1] = down[:, k * 128 : (k + 1) * 128] * SCALE
        for i, total in enumerate(across):
            rows_ref[i, m : m + 1] = jnp.sum(total.T, axis=0, keepdims=True) * SCALE
    for i in range(1, XN * YN):
        cols_ref[i] = cols_ref[0]


def multiply(features, total, parts):
    outs = [
        ((3, 2, ROWS, QUART), jnp.bfloat16),
        ((3, 2, ROWS, QUART), jnp.bfloat16),
        ((2, 3, ROWS), jnp.float32),
        ((XN * YN, 48, 128), jnp.float32),
    ]
    depth = TOKENS // 4
    scratch = [pltpu.VMEM((2, depth, QUART // 2), jnp.bfloat16)]
    return whole(multiply_kernel, "multiply", outs, (*features, total, *parts), 3 * 4 * ROWS * HALF * depth, scratch)


def span_kernel(parts_ref, old_ref, out_ref):
    total = parts_ref[0]
    for i in range(1, XN * YN):
        total += parts_ref[i]
    out_ref[...] = BETA * old_ref[...] + (1.0 - BETA) * (total * (1.0 / D) + EPS)


def weigh_kernel(rows_ref, met_ref, mine_ref, other_ref, keep_ref, got_ref, out_ref):
    out_ref[0, 0:3] = rows_ref[0] + met_ref[...]
    for m in range(3):
        total = jnp.zeros((ROWS, 128), jnp.float32)
        for ref, span_ref in ((keep_ref, mine_ref), (got_ref, other_ref)):
            for route in range(2):
                at = (m * 2 + route) * 8
                inverse = 1.0 / span_ref[at : at + 8]
                for k in range(8):
                    grad = ref[m, route, :, k * 128 : (k + 1) * 128].astype(jnp.float32)
                    total += grad * grad * inverse[k : k + 1]
        out_ref[0, 3 + m : 4 + m] = jnp.sum(total.T, axis=0, keepdims=True) * SCALE
    for i in range(1, ZN):
        out_ref[i] = out_ref[0]


def width_kernel(parts_ref, old_ref, width_ref, out_ref):
    total = parts_ref[0]
    for i in range(1, ZN):
        total += parts_ref[i]
    width = BETA * old_ref[...] + (1.0 - BETA) * (total[0:3] * (1.0 / FF) + EPS)
    width_ref[...] = width
    squares = total[3:6] / width
    squares = squares[:, :128] + squares[:, 128:]
    for i in range(XN * YN * CN):
        out_ref[i] = squares


def finish_kernel(core_ref, parts_ref, width_ref, mine_ref, other_ref, keep_ref, got_ref, *refs):
    outs, widths, spans, bufs, sem = refs[:3], refs[3:6], refs[6:9], refs[9:12], refs[12]
    core = core_ref[0]
    squares = parts_ref[0]
    for i in range(1, XN * YN * CN):
        squares += parts_ref[i]
    rms = jnp.sqrt(jnp.sum(squares, axis=1, keepdims=True) * (1.0 / (D * FF)))
    scaled = lax.rsqrt(width_ref[...]) * ((1.0 / 32.0) / jnp.maximum(1.0, rms))
    copies = []
    for m in range(3):
        widths[m][...] = width_ref[m : m + 1]
        width = jnp.broadcast_to(scaled[m : m + 1], (128, ROWS)).T
        for ref, span_ref, at in ((keep_ref, mine_ref, core), (got_ref, other_ref, 1 - core)):
            spans[m][pl.ds(pl.multiple_of(at * 16, 16), 16)] = span_ref[m * 16 : (m + 1) * 16]
            for route in range(2):
                first = at * HALF + route * QUART
                row = (m * 2 + route) * 8
                unit = lax.rsqrt(span_ref[row : row + 8])
                for k in range(8):
                    grad = ref[m, route, :, k * 128 : (k + 1) * 128].astype(jnp.float32)
                    normed = (grad * width * unit[k : k + 1]).astype(jnp.bfloat16)
                    place = pl.ds(pl.multiple_of(first + k * 128, 128), 128)
                    if m < 2:
                        bufs[m][:, place] = normed
                    else:
                        bufs[m][place, :] = normed.T
                part = pl.ds(pl.multiple_of(first, QUART), QUART)
                ends = [v.at[:, part] if m < 2 else v.at[part] for v in (bufs[m], outs[m])]
                copies.append(pltpu.make_async_copy(*ends, sem.at[len(copies)]))
                copies[-1].start()
    for copy in copies:
        copy.wait()


def finish(core, *operands):
    spec = pl.BlockSpec(memory_space=pltpu.VMEM)
    steps = [(ROWS, COLS), (ROWS, COLS), (COLS, ROWS)]
    operands = here(*operands)
    return pl.pallas_call(
        finish_kernel,
        in_specs=[pl.BlockSpec(memory_space=pltpu.SMEM)] + [spec] * len(operands),
        out_specs=[pl.BlockSpec(memory_space=pl.ANY)] * 3 + [spec] * 6,
        out_shape=[jax.ShapeDtypeStruct(shape, jnp.bfloat16) for shape in steps]
        + [jax.ShapeDtypeStruct((1, ROWS), jnp.float32)] * 3
        + [jax.ShapeDtypeStruct((COLS // 128, 128), jnp.float32)] * 3,
        scratch_shapes=[pltpu.VMEM(shape, jnp.bfloat16) for shape in steps] + [pltpu.SemaphoreType.DMA((12,))],
        compiler_params=pltpu.CompilerParams(vmem_limit_bytes=2 * VMEM),
        cost_estimate=pl.CostEstimate(flops=12 * ROWS * COLS, bytes_accessed=12 << 20, transcendentals=0),
        name="finish",
    )(core, *operands)


def arrange_kernel(place_ref, *refs):
    x, y, core, quarter = (place_ref[i] for i in range(4))
    sources, outs = refs[:4], refs[4:]
    for array in range(2):
        for part in range(4):
            slot = lax.rem(core + part // 2 + quarter // 2, 2)
            columns = slice(part % 2 * 128, (part % 2 + 1) * 128)
            rows = slice(part * 128, (part + 1) * 128)
            for route in range(2):
                for outer in range(4):
                    blocks = []
                    for inner in range(4):
                        dx, dy = (ORDER[outer], ORDER[inner]) if route else (ORDER[inner], ORDER[outer])
                        chip = lax.rem(x + dx, XN) * YN + lax.rem(y + dy, YN)
                        for own, met in (sources[:2], sources[2:]):
                            mine, theirs = (ref[slot, chip, :, columns] for ref in (own, met))
                            blocks.append(jnp.where(lax.rem(quarter, 2) == array, mine, theirs))
                    tokens = slice(outer * 256, (outer + 1) * 256)
                    outs[array * 2 + route][rows, tokens] = jnp.concatenate(blocks).T


def arrange(place, *sources):
    spec = pl.BlockSpec(memory_space=pltpu.VMEM)
    return pl.pallas_call(
        arrange_kernel,
        in_specs=[pl.BlockSpec(memory_space=pltpu.SMEM)] + [spec] * 4,
        out_specs=[spec] * 4,
        out_shape=[pltpu.VMEM((2 * ROWS, TOKENS), jnp.bfloat16)] * 4,
        compiler_params=pltpu.CompilerParams(vmem_limit_bytes=VMEM),
        cost_estimate=pl.CostEstimate(flops=0, bytes_accessed=6 << 20, transcendentals=0),
        name="arrange",
    )(place, *here(*sources))


def local(
    layer_input,
    output_grad,
    gate_pre,
    up_pre,
    hidden_grad,
    row_gate,
    col_gate,
    row_up,
    col_up,
    row_down,
    col_down,
):
    x, y, c, z = (lax.axis_index(name) for name in ("x", "y", "c", "z"))
    core = c.astype(jnp.int32).reshape(1)
    quarter = lax.rem(z, 4).astype(jnp.int32).reshape(1)
    place = jnp.stack((x, y, c, lax.rem(z, 4))).astype(jnp.int32)
    known = (core, quarter, place, c == 0, gate_pre, up_pre, hidden_grad)
    core, quarter, place, first, gate_pre, up_pre, hidden_grad = lax.optimization_barrier(known)
    old_span = jnp.stack((col_gate, col_up, row_down)).reshape(3, CN, 16, 128)
    old_span = jnp.where(first, old_span[:, 0], old_span[:, 1]).reshape(48, 128)
    old_width = jnp.stack((row_gate, row_up, col_down))

    def halves(at):
        return derive(*(lax.dynamic_slice_in_dim(v, at * HALF, HALF, 1) for v in (gate_pre, up_pre, hidden_grad)))

    got = swap(halves(1 - c))
    own = jnp.stack((halves(c), got))
    own_a, own_b = own[..., :QUART], own[..., QUART:]
    chosen = pick(quarter, layer_input, output_grad)
    own_a, own_b, chosen = lax.optimization_barrier((own_a, own_b, chosen))
    near = [neighbours(own_a, "x"), neighbours(own_b, "y")]
    chosen = lax.all_to_all(chosen, ("x", "y"), split_axis=0, concat_axis=0, tiled=True)
    near, old_span, old_width = lax.optimization_barrier((near, old_span, old_width))
    far = relay(near, ("x", "y"))
    far, chosen = lax.optimization_barrier((far, chosen))
    lines = join([own_a, *near[0], *far[0], own_b, *near[1], *far[1]])

    near = [neighbours(line, axis) for line, axis in zip(lines, ("y", "x"))]
    far = relay(near, ("y", "x"))
    chosen = jnp.stack((chosen, lax.ppermute(chosen, "z", [(i, i ^ 2) for i in range(ZN)])))
    met = lax.ppermute(chosen, "z", [(i, i ^ 1) for i in range(ZN)])
    features = arrange(place, chosen, met, swap(chosen), swap(met))
    parts = [lines[0], *near[0], lines[1], *near[1]]
    keep, send, rows, cols = multiply(features, start(features, parts), [*far[0], *far[1]])

    met = swap(rows[1])
    got = swap(send)

    parts = collect(cols, ("x", "y"))
    span = whole(span_kernel, "span", [((48, 128), jnp.float32)], (parts, old_span))[0]
    other = swap(span)
    sums = whole(weigh_kernel, "weigh", [((ZN, 6, ROWS), jnp.float32)], (rows, met, span, other, keep, got))[0]
    parts = collect(sums, ("z",))
    outs = [((3, ROWS), jnp.float32), ((XN * YN * CN, 3, 128), jnp.float32)]
    width, squares = whole(width_kernel, "width", outs, (parts, old_width))
    parts = collect(squares, ("x", "y", "c"))
    outs = finish(core, parts, width, span, other, keep, got)
    widths = [v.reshape(ROWS) for v in outs[3:6]]
    spans = [v.reshape(COLS) for v in outs[6:9]]
    return (*outs[:3], widths[0], spans[0], widths[1], spans[1], spans[2], widths[2])


def solution(mesh):
    grid = Mesh(mesh.devices.reshape(XN, YN, CN, ZN), ("x", "y", "c", "z"))
    dp = ("x", "y", "c")
    return jax.shard_map(
        local,
        mesh=grid,
        in_specs=(
            P(dp, None),
            P(dp, None),
            P(dp, "z"),
            P(dp, "z"),
            P(dp, "z"),
            P(dp),
            P("z"),
            P(dp),
            P("z"),
            P("z"),
            P(dp),
        ),
        out_specs=(
            P(dp, "z"),
            P(dp, "z"),
            P("z", dp),
            P(dp),
            P("z"),
            P(dp),
            P("z"),
            P("z"),
            P(dp),
        ),
        check_vma=False,
    )
```

```python
import jax
import jax.numpy as jnp
from jax import lax
from jax.experimental import pallas as pl
from jax.experimental.pallas import tpu as pltpu
from jax.sharding import Mesh, PartitionSpec as P

D = 8192
FF = 32768
STEP = 8
TOKENS = 1024

EPS = 1e-30
BETA = 1.0 - float(STEP) ** (-0.8)
XN, YN, CN, ZN = 4, 4, 2, 8
ROWS = D // (XN * YN * CN)
COLS = FF // ZN
HALF = COLS // 2
QUART = HALF // 2
LOCAL = TOKENS // (XN * YN * CN)
VMEM = 12 * 1024 * 1024
SCALE = 1.0 / TOKENS
ORDER = (0, 3, 1, 2)


def derive(gate_pre, up_pre, hidden_grad):
    first = gate_pre.astype(jnp.float32)
    second = up_pre.astype(jnp.float32)
    cotangent = hidden_grad.astype(jnp.float32)
    sigma = jax.nn.sigmoid(first)
    gate_cot = (cotangent * second * sigma * (1.0 + first * (1.0 - sigma))).astype(jnp.bfloat16)
    up_cot = (cotangent * first * sigma).astype(jnp.bfloat16)
    hidden = (first * sigma * second).astype(jnp.bfloat16)
    return jnp.stack((gate_cot, up_cot, hidden))


def shift(value, axis, size, step):
    return lax.ppermute(value, axis, [(i, (i + step) % size) for i in range(size)])


def swap(value):
    return shift(value, "c", CN, 1)


def neighbours(value, axis):
    return shift(value, axis, 4, 1), shift(value, axis, 4, 3)


def here(*values):
    return [pltpu.with_memory_space_constraint(v, pltpu.VMEM) for v in values]


def whole(kernel, name, outs, operands, flops=0, scratch=()):
    size = sum(v.size * v.dtype.itemsize for v in operands)
    spec = pl.BlockSpec(memory_space=pltpu.VMEM)
    return pl.pallas_call(
        kernel,
        in_specs=[spec] * len(operands),
        out_specs=[spec] * len(outs),
        out_shape=[pltpu.VMEM(shape, dtype) for shape, dtype in outs],
        scratch_shapes=list(scratch),
        compiler_params=pltpu.CompilerParams(vmem_limit_bytes=VMEM),
        cost_estimate=pl.CostEstimate(flops=flops, bytes_accessed=size, transcendentals=0),
        name=name,
    )(*here(*operands))


def halve_kernel(*refs):
    for i in range(4):
        half = refs[4 + i].shape[0]
        refs[4 + i][...] = refs[i][i % 2 * half : (i % 2 + 1) * half]


def relay(pairs, axes):
    arrived = [v for pair in pairs for v in pair]
    outs = [((v.shape[0] // 2,) + v.shape[1:], v.dtype) for v in arrived]
    halves = whole(halve_kernel, "halve", outs, arrived)
    return [(shift(halves[2 * r], axis, 4, 1), shift(halves[2 * r + 1], axis, 4, 3)) for r, axis in enumerate(axes)]


def collect(copies, axes):
    return lax.all_to_all(copies, axes, split_axis=0, concat_axis=0, tiled=True)


def join_kernel(*refs):
    for route in range(2):
        own, left, right, low, high = refs[5 * route : 5 * route + 5]
        line = refs[10 + route]
        for block, ref in enumerate((own, left, right)):
            line[block] = ref[...]
        line[3, 0] = low[0]
        line[3, 1] = high[0]


def join(blocks):
    return whole(join_kernel, "join", [((4, CN, 3, LOCAL, QUART), jnp.bfloat16)] * 2, blocks)


def pick_kernel(z_ref, first_ref, second_ref, out_ref, sem):
    for array, ref in enumerate((first_ref, second_ref)):

        @pl.when(lax.rem(z_ref[0], 2) == array)
        def _():
            copies = []
            for chip in range(XN * YN):
                start = pl.multiple_of((2 * chip + z_ref[0] // 2) * ROWS, ROWS)
                columns = ref.at[:, pl.ds(start, ROWS)]
                copies.append(pltpu.make_async_copy(columns, out_ref.at[chip], sem.at[chip]))
                copies[-1].start()
            for copy in copies:
                copy.wait()


def pick(z, first, second):
    return pl.pallas_call(
        pick_kernel,
        in_specs=[pl.BlockSpec(memory_space=pltpu.SMEM)] + [pl.BlockSpec(memory_space=pl.ANY)] * 2,
        out_specs=pl.BlockSpec(memory_space=pltpu.VMEM),
        out_shape=pltpu.VMEM((XN * YN, LOCAL, ROWS), jnp.bfloat16),
        scratch_shapes=[pltpu.SemaphoreType.DMA((XN * YN,))],
        compiler_params=pltpu.CompilerParams(vmem_limit_bytes=VMEM),
        cost_estimate=pl.CostEstimate(flops=0, bytes_accessed=1 << 20, transcendentals=0),
        name="pick",
    )(z, first, second)


def start_kernel(*refs):
    features, parts, total_ref, line = refs[:4], refs[4:10], refs[10], refs[11]
    depth = line.shape[1]
    tile = line.shape[2]
    for m in range(3):
        for step in range(QUART // tile):
            units = slice(step * tile, (step + 1) * tile)
            for route in range(2):
                x_ref = features[m // 2 * 2 + route]
                size = depth // 3
                for i, ref in enumerate(parts[3 * route : 3 * route + 3]):
                    line[route, i * size : (i + 1) * size] = ref[:, :, m, :, units].reshape(size, tile)
                for i in range(2):
                    rows = slice(i * ROWS, (i + 1) * ROWS)
                    total_ref[m, route, rows, units] = jnp.dot(
                        x_ref[rows, :depth], line[route], preferred_element_type=jnp.float32
                    )


def start(features, parts):
    outs = [((3, 2, 2 * ROWS, QUART), jnp.float32)]
    depth = TOKENS * 3 // 4
    scratch = [pltpu.VMEM((2, depth, QUART // 2), jnp.bfloat16)]
    return whole(start_kernel, "start", outs, (*features, *parts), 3 * 4 * ROWS * HALF * depth, scratch)[0]


def multiply_kernel(*refs):
    features, total_ref, parts = refs[:4], refs[4], refs[5:9]
    keep_ref, send_ref, cols_ref, line = refs[9:]
    depth = line.shape[1]
    tile = line.shape[2]
    for m in range(3):
        for step in range(QUART // tile):
            units = slice(step * tile, (step + 1) * tile)
            for route in range(2):
                x_ref = features[m // 2 * 2 + route]
                size = depth // 2
                for i, ref in enumerate(parts[2 * route : 2 * route + 2]):
                    line[route, i * size : (i + 1) * size] = ref[:, :, m, :, units].reshape(size, tile)
                down = jnp.zeros((1, tile), jnp.float32)
                for i, out_ref in enumerate((keep_ref, send_ref)):
                    rows = slice(i * ROWS, (i + 1) * ROWS)
                    last = jnp.dot(x_ref[rows, TOKENS - depth :], line[route], preferred_element_type=jnp.float32)
                    grad = total_ref[m, route, rows, units] + last
                    out_ref[m, route, :, units] = grad.astype(jnp.bfloat16)
                    square = grad * grad
                    down += jnp.sum(square, axis=0, keepdims=True)
                for k in range(tile // 128):
                    row = step * (tile // 128) + k
                    row += (m * 2 + route) * 8
                    cols_ref[0, row : row + 1] = down[:, k * 128 : (k + 1) * 128] * SCALE
    for i in range(1, XN * YN):
        cols_ref[i] = cols_ref[0]


def multiply(features, total, parts):
    outs = [
        ((3, 2, ROWS, QUART), jnp.bfloat16),
        ((3, 2, ROWS, QUART), jnp.bfloat16),
        ((XN * YN, 48, 128), jnp.float32),
    ]
    depth = TOKENS // 4
    scratch = [pltpu.VMEM((2, depth, QUART // 2), jnp.bfloat16)]
    return whole(multiply_kernel, "multiply", outs, (*features, total, *parts), 3 * 4 * ROWS * HALF * depth, scratch)


def span_kernel(parts_ref, old_ref, out_ref):
    total = parts_ref[0]
    for i in range(1, XN * YN):
        total += parts_ref[i]
    out_ref[...] = BETA * old_ref[...] + (1.0 - BETA) * (total * (1.0 / D) + EPS)


def weigh_kernel(mine_ref, other_ref, keep_ref, got_ref, out_ref):
    for m in range(3):
        total = jnp.zeros((ROWS, 128), jnp.float32)
        plain = jnp.zeros((ROWS, 128), jnp.float32)
        for ref, span_ref in ((keep_ref, mine_ref), (got_ref, other_ref)):
            for route in range(2):
                at = (m * 2 + route) * 8
                inverse = 1.0 / span_ref[at : at + 8]
                for k in range(8):
                    grad = ref[m, route, :, k * 128 : (k + 1) * 128].astype(jnp.float32)
                    square = grad * grad
                    plain += square
                    total += square * inverse[k : k + 1]
        out_ref[0, m : m + 1] = jnp.sum(plain.T, axis=0, keepdims=True) * SCALE
        out_ref[0, 3 + m : 4 + m] = jnp.sum(total.T, axis=0, keepdims=True) * SCALE
    for i in range(1, ZN):
        out_ref[i] = out_ref[0]


def width_kernel(parts_ref, old_ref, width_ref, out_ref):
    total = parts_ref[0]
    for i in range(1, ZN):
        total += parts_ref[i]
    width = BETA * old_ref[...] + (1.0 - BETA) * (total[0:3] * (1.0 / FF) + EPS)
    width_ref[...] = width
    squares = total[3:6] / width
    squares = squares[:, :128] + squares[:, 128:]
    for i in range(XN * YN * CN):
        out_ref[i] = squares


def finish_kernel(core_ref, parts_ref, width_ref, mine_ref, other_ref, keep_ref, got_ref, *refs):
    outs, widths, spans, bufs, sem = refs[:3], refs[3:6], refs[6:9], refs[9:12], refs[12]
    core = core_ref[0]
    squares = parts_ref[0]
    for i in range(1, XN * YN * CN):
        squares += parts_ref[i]
    rms = jnp.sqrt(jnp.sum(squares, axis=1, keepdims=True) * (1.0 / (D * FF)))
    scaled = lax.rsqrt(width_ref[...]) * ((1.0 / 32.0) / jnp.maximum(1.0, rms))
    copies = []
    for m in range(3):
        widths[m][...] = width_ref[m : m + 1]
        width = jnp.broadcast_to(scaled[m : m + 1], (128, ROWS)).T
        for ref, span_ref, at in ((keep_ref, mine_ref, core), (got_ref, other_ref, 1 - core)):
            spans[m][pl.ds(pl.multiple_of(at * 16, 16), 16)] = span_ref[m * 16 : (m + 1) * 16]
            for route in range(2):
                first = at * HALF + route * QUART
                row = (m * 2 + route) * 8
                unit = lax.rsqrt(span_ref[row : row + 8])
                for k in range(8):
                    grad = ref[m, route, :, k * 128 : (k + 1) * 128].astype(jnp.float32)
                    normed = (grad * width * unit[k : k + 1]).astype(jnp.bfloat16)
                    place = pl.ds(pl.multiple_of(first + k * 128, 128), 128)
                    if m < 2:
                        bufs[m][:, place] = normed
                    else:
                        bufs[m][place, :] = normed.T
                part = pl.ds(pl.multiple_of(first, QUART), QUART)
                ends = [v.at[:, part] if m < 2 else v.at[part] for v in (bufs[m], outs[m])]
                copies.append(pltpu.make_async_copy(*ends, sem.at[len(copies)]))
                copies[-1].start()
    for copy in copies:
        copy.wait()


def finish(core, *operands):
    spec = pl.BlockSpec(memory_space=pltpu.VMEM)
    steps = [(ROWS, COLS), (ROWS, COLS), (COLS, ROWS)]
    operands = here(*operands)
    return pl.pallas_call(
        finish_kernel,
        in_specs=[pl.BlockSpec(memory_space=pltpu.SMEM)] + [spec] * len(operands),
        out_specs=[pl.BlockSpec(memory_space=pl.ANY)] * 3 + [spec] * 6,
        out_shape=[jax.ShapeDtypeStruct(shape, jnp.bfloat16) for shape in steps]
        + [jax.ShapeDtypeStruct((1, ROWS), jnp.float32)] * 3
        + [jax.ShapeDtypeStruct((COLS // 128, 128), jnp.float32)] * 3,
        scratch_shapes=[pltpu.VMEM(shape, jnp.bfloat16) for shape in steps] + [pltpu.SemaphoreType.DMA((12,))],
        compiler_params=pltpu.CompilerParams(vmem_limit_bytes=2 * VMEM),
        cost_estimate=pl.CostEstimate(flops=12 * ROWS * COLS, bytes_accessed=12 << 20, transcendentals=0),
        name="finish",
    )(core, *operands)


def arrange_kernel(place_ref, *refs):
    x, y, core, quarter = (place_ref[i] for i in range(4))
    sources, outs = refs[:4], refs[4:]
    for array in range(2):
        for part in range(4):
            slot = lax.rem(core + part // 2 + quarter // 2, 2)
            columns = slice(part % 2 * 128, (part % 2 + 1) * 128)
            rows = slice(part * 128, (part + 1) * 128)
            for route in range(2):
                for outer in range(4):
                    blocks = []
                    for inner in range(4):
                        dx, dy = (ORDER[outer], ORDER[inner]) if route else (ORDER[inner], ORDER[outer])
                        chip = lax.rem(x + dx, XN) * YN + lax.rem(y + dy, YN)
                        for own, met in (sources[:2], sources[2:]):
                            mine, theirs = (ref[slot, chip, :, columns] for ref in (own, met))
                            blocks.append(jnp.where(lax.rem(quarter, 2) == array, mine, theirs))
                    tokens = slice(outer * 256, (outer + 1) * 256)
                    outs[array * 2 + route][rows, tokens] = jnp.concatenate(blocks).T


def arrange(place, *sources):
    spec = pl.BlockSpec(memory_space=pltpu.VMEM)
    return pl.pallas_call(
        arrange_kernel,
        in_specs=[pl.BlockSpec(memory_space=pltpu.SMEM)] + [spec] * 4,
        out_specs=[spec] * 4,
        out_shape=[pltpu.VMEM((2 * ROWS, TOKENS), jnp.bfloat16)] * 4,
        compiler_params=pltpu.CompilerParams(vmem_limit_bytes=VMEM),
        cost_estimate=pl.CostEstimate(flops=0, bytes_accessed=6 << 20, transcendentals=0),
        name="arrange",
    )(place, *here(*sources))


def local(
    layer_input,
    output_grad,
    gate_pre,
    up_pre,
    hidden_grad,
    row_gate,
    col_gate,
    row_up,
    col_up,
    row_down,
    col_down,
):
    x, y, c, z = (lax.axis_index(name) for name in ("x", "y", "c", "z"))
    core = c.astype(jnp.int32).reshape(1)
    quarter = lax.rem(z, 4).astype(jnp.int32).reshape(1)
    place = jnp.stack((x, y, c, lax.rem(z, 4))).astype(jnp.int32)
    known = (core, quarter, place, c == 0, gate_pre, up_pre, hidden_grad)
    core, quarter, place, first, gate_pre, up_pre, hidden_grad = lax.optimization_barrier(known)
    old_span = jnp.stack((col_gate, col_up, row_down)).reshape(3, CN, 16, 128)
    old_span = jnp.where(first, old_span[:, 0], old_span[:, 1]).reshape(48, 128)
    old_width = jnp.stack((row_gate, row_up, col_down))

    def halves(at):
        return derive(*(lax.dynamic_slice_in_dim(v, at * HALF, HALF, 1) for v in (gate_pre, up_pre, hidden_grad)))

    got = swap(halves(1 - c))
    own = jnp.stack((halves(c), got))
    own_a, own_b = own[..., :QUART], own[..., QUART:]
    chosen = pick(quarter, layer_input, output_grad)
    own_a, own_b, chosen = lax.optimization_barrier((own_a, own_b, chosen))
    near = [neighbours(own_a, "x"), neighbours(own_b, "y")]
    chosen = lax.all_to_all(chosen, ("x", "y"), split_axis=0, concat_axis=0, tiled=True)
    near, old_span, old_width = lax.optimization_barrier((near, old_span, old_width))
    far = relay(near, ("x", "y"))
    far, chosen = lax.optimization_barrier((far, chosen))
    lines = join([own_a, *near[0], *far[0], own_b, *near[1], *far[1]])

    near = [neighbours(line, axis) for line, axis in zip(lines, ("y", "x"))]
    far = relay(near, ("y", "x"))
    chosen = jnp.stack((chosen, lax.ppermute(chosen, "z", [(i, i ^ 2) for i in range(ZN)])))
    met = lax.ppermute(chosen, "z", [(i, i ^ 1) for i in range(ZN)])
    features = arrange(place, chosen, met, swap(chosen), swap(met))
    parts = [lines[0], *near[0], lines[1], *near[1]]
    keep, send, cols = multiply(features, start(features, parts), [*far[0], *far[1]])

    got = swap(send)

    parts = collect(cols, ("x", "y"))
    span = whole(span_kernel, "span", [((48, 128), jnp.float32)], (parts, old_span))[0]
    other = swap(span)
    sums = whole(weigh_kernel, "weigh", [((ZN, 6, ROWS), jnp.float32)], (span, other, keep, got))[0]
    parts = collect(sums, ("z",))
    outs = [((3, ROWS), jnp.float32), ((XN * YN * CN, 3, 128), jnp.float32)]
    width, squares = whole(width_kernel, "width", outs, (parts, old_width))
    parts = collect(squares, ("x", "y", "c"))
    outs = finish(core, parts, width, span, other, keep, got)
    widths = [v.reshape(ROWS) for v in outs[3:6]]
    spans = [v.reshape(COLS) for v in outs[6:9]]
    return (*outs[:3], widths[0], spans[0], widths[1], spans[1], spans[2], widths[2])


def solution(mesh):
    grid = Mesh(mesh.devices.reshape(XN, YN, CN, ZN), ("x", "y", "c", "z"))
    dp = ("x", "y", "c")
    return jax.shard_map(
        local,
        mesh=grid,
        in_specs=(
            P(dp, None),
            P(dp, None),
            P(dp, "z"),
            P(dp, "z"),
            P(dp, "z"),
            P(dp),
            P("z"),
            P(dp),
            P("z"),
            P("z"),
            P(dp),
        ),
        out_specs=(
            P(dp, "z"),
            P(dp, "z"),
            P("z", dp),
            P(dp),
            P("z"),
            P(dp),
            P("z"),
            P("z"),
            P(dp),
        ),
        check_vma=False,
    )
```
